128 devices in a mesh: dp: 8 (over z_hi, y), blk: 2 (over z_lo), ulysses: 8 (over x, core).
Axes of the slice: x: 4, y: 4, z: 4 (z_hi: 2, z_lo: 2; z = z_hi * 2 + z_lo), core: 2. Of those that a mesh axis runs over, the one named last changes fastest.
Arguments:
- video_query: bfloat16 [32768, 3072], P(('dp', 'blk', 'ulysses')), parts along dimension 0, may hold values from -20 to 20
- video_key: bfloat16 [32768, 3072], P(('dp', 'blk', 'ulysses')), parts along dimension 0, may hold values from -20 to 20
- video_value: bfloat16 [32768, 3072], P(('dp', 'blk', 'ulysses')), parts along dimension 0, may hold values from -6 to 6
- text_query: bfloat16 [2048, 3072], P(('dp', 'ulysses')), parts along dimension 0, may hold values from -20 to 20
- text_key: bfloat16 [2048, 3072], P(('dp', 'ulysses')), parts along dimension 0, may hold values from -6 to 6
- text_value: bfloat16 [2048, 3072], P(('dp', 'ulysses')), parts along dimension 0, may hold values from -6 to 6
- text_length: int32 [8], P('dp'), parts along dimension 0, may hold values from 64 to 256
Outputs:
- video_out: bfloat16 [32768, 3072], P(('dp', 'blk', 'ulysses')), parts along dimension 0
- text_out: bfloat16 [2048, 3072], P(('dp', 'blk', 'ulysses')), parts along dimension 0
The draws below stay inside these ranges and needn't reach their ends.
There are 8 independent parts, one for each index of `dp`. The reference program is written for one: setup_inputs(seed, part) draws one part's arguments, and reference() takes and returns one part's arrays. A program takes and returns all parts, laid end to end along the dimension named above; each array names one. Nothing has to cross between parts.
All inputs are finite; a program needn't handle non-finite values.
Results may differ from the reference program's by a relative error of at most 0.009.
Values may be sent and summed in bfloat16 or wider, within the bound.
A program may use at most 128 MiB of HBM per device.

```python
import jax
import jax.numpy as jnp
from jax import lax

HEADS = 24
HEAD_DIM = 128
D = 3072
TEXT = 256
VIDEO = 4096


def draw_video_key(key, part):
    key = jax.random.fold_in(key, 7)
    drawn = jnp.clip(jax.random.normal(key, (VIDEO, D), jnp.float32), -6.0, 6.0)
    return drawn.astype(jnp.bfloat16)


def draw_video_query(key, part):
    key = jax.random.fold_in(key, 11)
    drawn = jnp.clip(jax.random.normal(key, (VIDEO, D), jnp.float32), -6.0, 6.0)
    return drawn.astype(jnp.bfloat16)


def draw_text_query(key, part):
    key = jax.random.fold_in(key, 13)
    drawn = jnp.clip(jax.random.normal(key, (TEXT, D), jnp.float32), -6.0, 6.0)
    return drawn.astype(jnp.bfloat16)


def block_levels(rng, extent, cuts, least, largest):
    def one(dim, parts):
        steps = jax.random.uniform(jax.random.fold_in(jax.random.fold_in(rng, 6), dim), (parts,), jnp.float32, least / len(cuts), largest / len(cuts))
        return jnp.repeat(jnp.exp(steps), extent[dim] // parts).reshape((-1,) + (1,) * (len(extent) - dim - 1))

    factor_of = one(*cuts[0])
    for cut in cuts[1:]:
        factor_of = factor_of * one(*cut)
    return factor_of


def bell_draw(own_key, extent, spread, most, pieces=(), kind=jnp.bfloat16):
    result = jax.random.normal(own_key, extent, jnp.float32) * spread
    if len(pieces) > 0:
        result = block_levels(own_key, extent, pieces, -0.22, 0.18) * result
    return jnp.clip(result, min=-most, max=most).astype(kind)


def setup_inputs(seed: int = 0, part: int = 0) -> dict:
    key_list = jax.random.split(jax.random.key(seed), 8)
    part_keys = jax.random.split(jax.random.fold_in(key_list[7], part), 8)
    video_query = draw_video_query(jax.random.fold_in(jax.random.fold_in(key_list[7], part), 71), part)
    video_key = draw_video_key(jax.random.fold_in(jax.random.fold_in(key_list[7], part), 71), part)
    video_value = bell_draw(part_keys[2], (VIDEO, D), 1.0, 6.0, ((0, 16),))
    text_query = draw_text_query(jax.random.fold_in(jax.random.fold_in(key_list[7], part), 71), part)
    text_key = bell_draw(part_keys[4], (TEXT, D), 1.0, 6.0, ((0, 8),))
    text_value = bell_draw(part_keys[5], (TEXT, D), 1.0, 6.0, ((0, 8),))
    text_length = jax.random.randint(part_keys[6], (1,), TEXT // 4, TEXT + 1).astype(jnp.int32)
    return dict(video_query=video_query, video_key=video_key, video_value=video_value, text_query=text_query, text_key=text_key, text_value=text_value, text_length=text_length)


def reference(video_query, video_key, video_value, text_query, text_key, text_value, text_length):
    queries = jnp.concatenate([video_query, text_query], axis=0)
    keys = jnp.concatenate([video_key, text_key], axis=0)
    values = jnp.concatenate([video_value, text_value], axis=0)
    rows = queries.shape[0]
    position = jnp.arange(keys.shape[0], dtype=jnp.int32)
    valid = (position < VIDEO) | (position - VIDEO < text_length[0])
    scale = HEAD_DIM ** -0.5
    qh = queries.reshape(rows, HEADS, HEAD_DIM).transpose(1, 0, 2)
    kh = keys.reshape(rows, HEADS, HEAD_DIM).transpose(1, 0, 2)
    vh = values.reshape(rows, HEADS, HEAD_DIM).transpose(1, 0, 2)

    def one_head(triple):
        qq, kk, vv = triple
        scores = jnp.dot(qq, kk.T, preferred_element_type=jnp.float32) * scale
        scores = jnp.where(valid[None, :], scores, jnp.float32(-1e30))
        top = jnp.max(scores, axis=-1, keepdims=True)
        weights = jnp.where(valid[None, :], jnp.exp(scores - top), jnp.float32(0.0))
        total = jnp.sum(weights, axis=-1, keepdims=True)
        summed = jnp.dot(weights.astype(jnp.bfloat16), vv, preferred_element_type=jnp.float32)
        return summed / total

    attended = lax.map(one_head, (qh, kh, vh))
    attended = attended.transpose(1, 0, 2).reshape(rows, HEADS * HEAD_DIM).astype(jnp.bfloat16)
    return attended[:VIDEO], attended[VIDEO:]
```

```python
import math

import jax
import jax.numpy as jnp
from jax import lax
from jax.experimental import pallas as pl
from jax.experimental.pallas import tpu as pltpu
from jax.sharding import PartitionSpec as P

MESH = pl.DeviceIdType.MESH
HEAD = 128
NEG_BIG = -1e30
SCALE = HEAD ** -0.5 * math.log2(math.e)
XS, ZS, CORES = 4, 2, 2
CHIPS = XS * ZS
HEADS_HERE = 3
ROWS = 256
TEXT_ROWS = 32
OUT_TEXT = 16
HALF = CHIPS * ROWS + XS * TEXT_ROWS
KEYS = CORES * HALF
PAIR = ZS * ROWS + TEXT_ROWS
PEERS = ((1, 0), (3, 0), (2, 0), (0, 1), (1, 1), (3, 1), (2, 1))
VIDEO_1 = CHIPS * ROWS + CORES * XS * TEXT_ROWS
BLOCKS = (
    (CHIPS * ROWS, VIDEO_1),
    (0, 1024),
    (1024, 2048),
    (VIDEO_1, VIDEO_1 + 1024),
    (VIDEO_1 + 1024, VIDEO_1 + 2048),
)


def dot(a, b, dims):
    return lax.dot_general(a, b, (dims, ((), ())), preferred_element_type=jnp.float32)


def wait_for(ref, sem):
    pltpu.make_async_copy(ref, ref, sem).wait()


def kernel(
    length, vq, vk, vv, tq, tk, tv, vo, to,
    keys, values, queries, outs,
    recv, send, sib_recv, sib_send, out_recv, out_send, text_recv, text_send,
):
    u = lax.axis_index("ulysses")
    z = lax.axis_index("blk")
    x, c = u // CORES, lax.rem(u, CORES)
    me = z * (XS * CORES) + u

    def device(px, pz, pc):
        return {"blk": pz, "ulysses": px * CORES + pc}

    barrier = pltpu.get_barrier_semaphore()
    for step in range(1, CHIPS * CORES):
        other = lax.rem(me + step, CHIPS * CORES)
        pl.semaphore_signal(
            barrier,
            inc=1,
            device_id={"blk": other // (XS * CORES), "ulysses": lax.rem(other, XS * CORES)},
            device_id_type=MESH,
        )
    pl.semaphore_wait(barrier, CHIPS * CORES - 1)

    def columns(px, pz, h):
        return pl.ds(pl.multiple_of(((px * ZS + pz) * HEADS_HERE + h) * HEAD, HEAD), HEAD)

    chip = x * ZS + z
    key_rows = pl.ds(pl.multiple_of(c * VIDEO_1 + chip * ROWS, 16), ROWS)
    key_text = pl.ds(
        pl.multiple_of(CHIPS * ROWS + c * (XS * TEXT_ROWS) + x * TEXT_ROWS, 16), TEXT_ROWS
    )
    query_rows = pl.ds(pl.multiple_of(x * PAIR + z * ROWS, 16), ROWS)
    query_text = pl.ds(pl.multiple_of(x * PAIR + ZS * ROWS, 16), TEXT_ROWS)
    mine = pl.ds(pl.multiple_of(c * HALF, 16), HALF)
    theirs = pl.ds(pl.multiple_of((1 - c) * HALF, 16), HALF)
    lanes = pl.ds(0, HEAD)

    def scatter(h, carry):
        for i, (video, text, place, rows, text_rows) in enumerate(
            (
                (vk, tk, keys, key_rows, key_text),
                (vv, tv, values, key_rows, key_text),
                (vq, tq, queries, query_rows, query_text),
            )
        ):
            land = place.at[h, rows, lanes]
            land_text = place.at[h, text_rows, lanes]
            for dx, dz in PEERS:
                px, pz = lax.rem(x + dx, XS), lax.rem(z + dz, ZS)
                pltpu.make_async_remote_copy(
                    src_ref=video.at[:, columns(px, pz, h)],
                    dst_ref=land,
                    send_sem=send.at[i, h],
                    recv_sem=recv.at[i, h],
                    device_id=device(px, pz, c),
                    device_id_type=MESH,
                ).start()
                if dz == 0:
                    pltpu.make_async_remote_copy(
                        src_ref=text.at[:, columns(px, pz, h)],
                        dst_ref=land_text,
                        send_sem=send.at[i, h],
                        recv_sem=recv.at[i, h],
                        device_id=device(px, pz, c),
                        device_id_type=MESH,
                    ).start()
            pltpu.make_async_copy(video.at[:, columns(x, z, h)], land, recv.at[i, h]).start()
            pltpu.make_async_copy(text.at[:, columns(x, z, h)], land_text, recv.at[i, h]).start()
        return carry

    lax.fori_loop(0, HEADS_HERE, scatter, 0)

    for h in range(HEADS_HERE):
        values[h, :, HEAD:] = jnp.ones((KEYS, HEAD), jnp.bfloat16)

    def to_sibling(i, place, h):
        wait_for(place.at[h, mine, lanes], recv.at[i, h])
        pltpu.make_async_remote_copy(
            src_ref=place.at[h, mine, lanes],
            dst_ref=place.at[h, mine, lanes],
            send_sem=sib_send.at[i, h],
            recv_sem=sib_recv.at[i, h],
            device_id=device(x, z, 1 - c),
            device_id_type=MESH,
        ).start()

    def attend(h, b):
        rows = pl.ds(pl.multiple_of(b * PAIR, 16), PAIR)
        q = queries[h, rows, :]
        t = lax.broadcasted_iota(jnp.int32, (1, CORES * XS * TEXT_ROWS), 1)
        part = XS * TEXT_ROWS
        position = (
            (lax.rem(t, part) // TEXT_ROWS) * (CORES * TEXT_ROWS)
            + (t // part) * TEXT_ROWS
            + lax.rem(t, TEXT_ROWS)
        )
        valid = position < length[0]
        top = None
        first, last = BLOCKS[0]
        scores = dot(q, keys[h, first:last, :], ((1,), (1,)))
        scores = jnp.where(valid, scores, NEG_BIG)
        for j, (first, last) in enumerate(BLOCKS):
            if j + 1 < len(BLOCKS):
                lo, hi = BLOCKS[j + 1]
                following = dot(q, keys[h, lo:hi, :], ((1,), (1,)))
            here = jnp.max(scores, axis=1, keepdims=True)
            new_top = here if top is None else jnp.maximum(top, here)
            weights = jnp.exp2(scores * SCALE - new_top * SCALE).astype(jnp.bfloat16)
            product = dot(weights, values[h, first:last, :], ((1,), (0,)))
            if top is None:
                summed = product
            else:
                summed = summed * jnp.exp2((top - new_top) * SCALE) + product
            top = new_top
            if j + 1 < len(BLOCKS):
                scores = following
        outs[h, rows, :] = (summed[:, :HEAD] / summed[:, HEAD:]).astype(jnp.bfloat16)

    def video_back(h, b, pz):
        return pltpu.make_async_remote_copy(
            src_ref=outs.at[h, pl.ds(pl.multiple_of(b * PAIR + pz * ROWS, 16), ROWS), :],
            dst_ref=vo.at[:, columns(x, z, h)],
            send_sem=out_send.at[h],
            recv_sem=out_recv,
            device_id=device(b, pz, c),
            device_id_type=MESH,
        )

    def text_place(h, b, k):
        src = outs.at[
            h, pl.ds(pl.multiple_of(b * PAIR + ZS * ROWS + k * OUT_TEXT, 16), OUT_TEXT), :
        ]
        px, pz = lax.rem(b * CORES + c, XS), (b * CORES + c) // XS
        own = (px == x) & (pz == z) & (c == k)
        return src, to.at[:, columns(x, z, h)], px, pz, own

    def text_back(h, b, k):
        src, dst, px, pz, own = text_place(h, b, k)
        return own, pltpu.make_async_remote_copy(
            src_ref=src,
            dst_ref=dst,
            send_sem=text_send.at[h],
            recv_sem=text_recv,
            device_id=device(px, pz, k),
            device_id_type=MESH,
        )

    to_sibling(0, keys, 0)
    to_sibling(1, values, 0)

    def turn(t, carry):
        h, i = t // XS, lax.rem(t, XS)
        b = lax.rem(x + 1 + i, XS)

        @pl.when(i == 0)
        def _():
            wait_for(queries.at[h], recv.at[2, h])
            wait_for(keys.at[h, theirs, lanes], sib_recv.at[0, h])
            wait_for(values.at[h, theirs, lanes], sib_recv.at[1, h])

        @pl.when((i == XS - 1) & (h < HEADS_HERE - 1))
        def _():
            to_sibling(0, keys, h + 1)

        attend(h, b)

        for dz in (1, 0):
            pz = lax.rem(z + dz, ZS)
            if dz == 1:
                video_back(h, b, pz).start()
            else:

                @pl.when(i < XS - 1)
                def _():
                    video_back(h, b, pz).start()

                @pl.when(i == XS - 1)
                def _():
                    pltpu.make_async_copy(
                        outs.at[h, query_rows, :], vo.at[:, columns(x, z, h)], out_recv
                    ).start()

        for k in range(CORES):
            own, copy = text_back(h, b, k)
            src, dst, _, _, _ = text_place(h, b, k)

            @pl.when(own)
            def _():
                pltpu.make_async_copy(src, dst, text_recv).start()

            @pl.when(jnp.logical_not(own))
            def _():
                copy.start()

        @pl.when((i == XS - 1) & (h < HEADS_HERE - 1))
        def _():
            to_sibling(1, values, h + 1)

        return carry

    lax.fori_loop(0, HEADS_HERE * XS, turn, 0)

    def finish(h, carry):
        for i in range(3):
            sent = (CHIPS - 1) * ROWS + (XS - 1) * TEXT_ROWS
            wait_for(outs.at[h, pl.ds(0, sent), :], send.at[i, h])
        for i, place in ((0, keys), (1, values)):
            wait_for(place.at[h, mine, lanes], sib_send.at[i, h])
        wait_for(outs.at[h, pl.ds(0, (CHIPS - 1) * ROWS), :], out_send.at[h])
        for b in range(XS):
            for k in range(CORES):
                own, copy = text_back(h, b, k)

                @pl.when(jnp.logical_not(own))
                def _():
                    copy.wait_send()

        return carry

    lax.fori_loop(0, HEADS_HERE, finish, 0)
    wait_for(vo, out_recv)
    wait_for(to, text_recv)


def on_device(video_query, video_key, video_value, text_query, text_key, text_value, text_length):
    any_spec = pl.BlockSpec(memory_space=pl.ANY)
    dma = pltpu.SemaphoreType.DMA
    width = video_query.shape[1]
    flops = 4 * HEADS_HERE * XS * PAIR * KEYS * HEAD
    return pl.pallas_call(
        kernel,
        out_shape=(
            jax.ShapeDtypeStruct((ROWS, width), jnp.bfloat16),
            jax.ShapeDtypeStruct((OUT_TEXT, width), jnp.bfloat16),
        ),
        in_specs=[pl.BlockSpec(memory_space=pltpu.SMEM)] + [any_spec] * 6,
        out_specs=(any_spec, any_spec),
        scratch_shapes=[
            pltpu.VMEM((HEADS_HERE, KEYS, HEAD), jnp.bfloat16),
            pltpu.VMEM((HEADS_HERE, KEYS, 2 * HEAD), jnp.bfloat16),
            pltpu.VMEM((HEADS_HERE, XS * PAIR, HEAD), jnp.bfloat16),
            pltpu.VMEM((HEADS_HERE, XS * PAIR, HEAD), jnp.bfloat16),
            dma((3, HEADS_HERE)),
            dma((3, HEADS_HERE)),
            dma((2, HEADS_HERE)),
            dma((2, HEADS_HERE)),
            dma,
            dma((HEADS_HERE,)),
            dma,
            dma((HEADS_HERE,)),
        ],
        cost_estimate=pl.CostEstimate(
            flops=flops, bytes_accessed=8 * ROWS * width, transcendentals=flops // (4 * HEAD)
        ),
        compiler_params=pltpu.CompilerParams(
            collective_id=0, has_side_effects=True, vmem_limit_bytes=52 * 2**20
        ),
        name="joint_attention",
    )(text_length, video_query, video_key, video_value, text_query, text_key, text_value)


def solution(mesh):
    assert mesh.shape["blk"] == ZS and mesh.shape["ulysses"] == XS * CORES
    tokens = P(("dp", "blk", "ulysses"), None)
    text = P(("dp", "ulysses"), None)
    return jax.shard_map(
        on_device,
        mesh=mesh,
        in_specs=(tokens, tokens, tokens, text, text, text, P("dp")),
        out_specs=(tokens, tokens),
        check_vma=False,
    )
```

```python
import math

import jax
import jax.numpy as jnp
from jax import lax
from jax.experimental import pallas as pl
from jax.experimental.pallas import tpu as pltpu
from jax.sharding import PartitionSpec as P

MESH = pl.DeviceIdType.MESH
HEAD = 128
NEG_BIG = -1e30
SCALE = HEAD ** -0.5 * math.log2(math.e)
XS, ZS, CORES = 4, 2, 2
CHIPS = XS * ZS
HEADS_HERE = 3
ROWS = 256
TEXT_ROWS = 32
OUT_TEXT = 16
HALF = CHIPS * ROWS + XS * TEXT_ROWS
KEYS = CORES * HALF
PAIR = ZS * ROWS + TEXT_ROWS
PEERS = ((1, 0), (3, 0), (2, 0), (0, 1), (1, 1), (3, 1), (2, 1))
QUERY_PEERS = ((3, 0), (3, 1), (2, 0), (2, 1), (1, 0), (1, 1), (0, 1))
VIDEO_1 = CHIPS * ROWS + CORES * XS * TEXT_ROWS
BLOCKS = (
    (CHIPS * ROWS, VIDEO_1),
    (0, 1024),
    (1024, 2048),
    (VIDEO_1, VIDEO_1 + 1024),
    (VIDEO_1 + 1024, VIDEO_1 + 2048),
)


def dot(a, b, dims):
    return lax.dot_general(a, b, (dims, ((), ())), preferred_element_type=jnp.float32)


def wait_for(ref, sem):
    pltpu.make_async_copy(ref, ref, sem).wait()


def kernel(
    length_in, vq, vk, vv, tq, tk, tv, vo, to,
    keys, values, queries, outs, staged, length, length_sem, stage_send, stage_recv,
    recv, query_recv, send, sib_recv, sib_send, out_recv, out_send, text_recv, text_send,
):
    u = lax.axis_index("ulysses")
    z = lax.axis_index("blk")
    x, c = u // CORES, lax.rem(u, CORES)

    def device(px, pz, pc):
        return {"blk": pz, "ulysses": px * CORES + pc}

    length_copy = pltpu.make_async_copy(length_in, length, length_sem)
    length_copy.start()

    barrier = pltpu.get_barrier_semaphore()
    for dx, dz in PEERS:
        pl.semaphore_signal(
            barrier,
            inc=1,
            device_id=device(lax.rem(x + dx, XS), lax.rem(z + dz, ZS), c),
            device_id_type=MESH,
        )
    pl.semaphore_signal(barrier, inc=1, device_id=device(x, z, 1 - c), device_id_type=MESH)
    pl.semaphore_wait(barrier, CHIPS)

    def columns(px, pz, h):
        return pl.ds(pl.multiple_of(((px * ZS + pz) * HEADS_HERE + h) * HEAD, HEAD), HEAD)

    chip = x * ZS + z
    key_rows = pl.ds(pl.multiple_of(c * VIDEO_1 + chip * ROWS, 16), ROWS)
    key_text = pl.ds(
        pl.multiple_of(CHIPS * ROWS + c * (XS * TEXT_ROWS) + x * TEXT_ROWS, 16), TEXT_ROWS
    )
    query_rows = pl.ds(pl.multiple_of(x * PAIR + z * ROWS, 16), ROWS)
    own_text = pl.ds(pl.multiple_of(x * PAIR + ZS * ROWS + c * OUT_TEXT, 16), OUT_TEXT)
    other_text = pl.ds(pl.multiple_of(x * PAIR + ZS * ROWS + (1 - c) * OUT_TEXT, 16), OUT_TEXT)
    mine = pl.ds(pl.multiple_of(c * HALF, 16), HALF)
    theirs = pl.ds(pl.multiple_of((1 - c) * HALF, 16), HALF)
    lanes = pl.ds(0, HEAD)

    stage = pltpu.make_async_remote_copy(
        src_ref=tq.at[pl.ds(pl.multiple_of((1 - c) * OUT_TEXT, 16), OUT_TEXT), :],
        dst_ref=staged,
        send_sem=stage_send,
        recv_sem=stage_recv,
        device_id=device(x, z, 1 - c),
        device_id_type=MESH,
    )
    stage.start()

    def scatter(h, pieces, dst, sems, peers):
        for dx, dz in peers:
            px, pz = lax.rem(x + dx, XS), lax.rem(z + dz, ZS)
            pltpu.make_async_remote_copy(
                src_ref=pieces.at[:, columns(px, pz, h)],
                dst_ref=dst,
                send_sem=sems[0],
                recv_sem=sems[1],
                device_id=device(px, pz, c),
                device_id_type=MESH,
            ).start()
        pltpu.make_async_copy(pieces.at[:, columns(x, z, h)], dst, sems[1]).start()

    text_peers = tuple(p for p in PEERS if p[1] == 0)
    tq_own = tq.at[pl.ds(pl.multiple_of(c * OUT_TEXT, 16), OUT_TEXT), :]

    def scatter_head(h, carry):
        for i, (video, text, place) in enumerate(((vk, tk, keys), (vv, tv, values))):
            sems = send.at[i, h], recv.at[i, h]
            scatter(h, video, place.at[h, key_rows, lanes], sems, PEERS)
            scatter(h, text, place.at[h, key_text, lanes], sems, text_peers)
        sems = send.at[2, h], query_recv.at[h, x]
        scatter(h, vq, queries.at[h, query_rows, :], sems, QUERY_PEERS)

        @pl.when(h == 0)
        def _():
            stage.wait()

        scatter(h, tq_own, queries.at[h, own_text, :], sems, text_peers)
        scatter(h, staged, queries.at[h, other_text, :], sems, text_peers)
        return carry

    lax.fori_loop(0, HEADS_HERE, scatter_head, 0)

    for h in range(HEADS_HERE):
        values[h, :, HEAD:] = jnp.ones((KEYS, HEAD), jnp.bfloat16)

    def to_sibling(i, place, h):
        wait_for(place.at[h, mine, lanes], recv.at[i, h])
        pltpu.make_async_remote_copy(
            src_ref=place.at[h, mine, lanes],
            dst_ref=place.at[h, mine, lanes],
            send_sem=sib_send.at[i, h],
            recv_sem=sib_recv.at[i, h],
            device_id=device(x, z, 1 - c),
            device_id_type=MESH,
        ).start()

    def attend(h, b):
        rows = pl.ds(pl.multiple_of(b * PAIR, 16), PAIR)
        q = queries[h, rows, :]
        t = lax.broadcasted_iota(jnp.int32, (1, CORES * XS * TEXT_ROWS), 1)
        part = XS * TEXT_ROWS
        position = (
            (lax.rem(t, part) // TEXT_ROWS) * (CORES * TEXT_ROWS)
            + (t // part) * TEXT_ROWS
            + lax.rem(t, TEXT_ROWS)
        )
        valid = position < length[0]
        top = None
        first, last = BLOCKS[0]
        scores = dot(q, keys[h, first:last, :], ((1,), (1,)))
        scores = jnp.where(valid, scores, NEG_BIG)
        for j, (first, last) in enumerate(BLOCKS):
            if j + 1 < len(BLOCKS):
                lo, hi = BLOCKS[j + 1]
                following = dot(q, keys[h, lo:hi, :], ((1,), (1,)))
            here = jnp.max(scores, axis=1, keepdims=True)
            new_top = here if top is None else jnp.maximum(top, here)
            weights = jnp.exp2(scores * SCALE - new_top * SCALE).astype(jnp.bfloat16)
            product = dot(weights, values[h, first:last, :], ((1,), (0,)))
            if top is None:
                summed = product
            else:
                summed = summed * jnp.exp2((top - new_top) * SCALE) + product
            top = new_top
            if j + 1 < len(BLOCKS):
                scores = following
        outs[h, rows, :] = (summed[:, :HEAD] / summed[:, HEAD:]).astype(jnp.bfloat16)

    def video_back(h, b, pz):
        return pltpu.make_async_remote_copy(
            src_ref=outs.at[h, pl.ds(pl.multiple_of(b * PAIR + pz * ROWS, 16), ROWS), :],
            dst_ref=vo.at[:, columns(x, z, h)],
            send_sem=out_send.at[h],
            recv_sem=out_recv,
            device_id=device(b, pz, c),
            device_id_type=MESH,
        )

    def text_place(h, b, k):
        src = outs.at[
            h, pl.ds(pl.multiple_of(b * PAIR + ZS * ROWS + k * OUT_TEXT, 16), OUT_TEXT), :
        ]
        px, pz = lax.rem(b, ZS) * CORES + k, b // ZS
        return src, to.at[:, columns(x, z, h)], px, pz, (px == x) & (pz == z)

    def text_back(h, b, k):
        src, dst, px, pz, own = text_place(h, b, k)
        return own, pltpu.make_async_remote_copy(
            src_ref=src,
            dst_ref=dst,
            send_sem=text_send.at[h],
            recv_sem=text_recv,
            device_id=device(px, pz, c),
            device_id_type=MESH,
        )

    length_copy.wait()
    to_sibling(0, keys, 0)
    to_sibling(1, values, 0)

    def turn(t, carry):
        h, i = t // XS, lax.rem(t, XS)
        b = lax.rem(x + 1 + i, XS)

        wait_for(
            queries.at[h, pl.ds(pl.multiple_of(b * PAIR, 16), PAIR), :], query_recv.at[h, b]
        )

        @pl.when(i == 0)
        def _():
            wait_for(keys.at[h, theirs, lanes], sib_recv.at[0, h])
            wait_for(values.at[h, theirs, lanes], sib_recv.at[1, h])

        @pl.when((i == XS - 1) & (h < HEADS_HERE - 1))
        def _():
            to_sibling(0, keys, h + 1)

        attend(h, b)

        for dz in (1, 0):
            pz = lax.rem(z + dz, ZS)
            if dz == 1:
                video_back(h, b, pz).start()
            else:

                @pl.when(i < XS - 1)
                def _():
                    video_back(h, b, pz).start()

                @pl.when(i == XS - 1)
                def _():
                    pltpu.make_async_copy(
                        outs.at[h, query_rows, :], vo.at[:, columns(x, z, h)], out_recv
                    ).start()

        for k in range(CORES):
            own, copy = text_back(h, b, k)
            src, dst, _, _, _ = text_place(h, b, k)

            @pl.when(own)
            def _():
                pltpu.make_async_copy(src, dst, text_recv).start()

            @pl.when(jnp.logical_not(own))
            def _():
                copy.start()

        @pl.when((i == XS - 1) & (h < HEADS_HERE - 1))
        def _():
            to_sibling(1, values, h + 1)

        return carry

    lax.fori_loop(0, HEADS_HERE * XS, turn, 0)

    def finish(h, carry):
        for i in range(3):
            sent = (CHIPS - 1) * ROWS + (XS - 1) * TEXT_ROWS
            wait_for(outs.at[h, pl.ds(0, sent), :], send.at[i, h])
        for i, place in ((0, keys), (1, values)):
            wait_for(place.at[h, mine, lanes], sib_send.at[i, h])
        wait_for(outs.at[h, pl.ds(0, (CHIPS - 1) * ROWS), :], out_send.at[h])
        for b in range(XS):
            for k in range(CORES):
                own, copy = text_back(h, b, k)

                @pl.when(jnp.logical_not(own))
                def _():
                    copy.wait_send()

        return carry

    lax.fori_loop(0, HEADS_HERE, finish, 0)
    wait_for(vo, out_recv)
    wait_for(to, text_recv)


def copy_out(video, text, video_out, text_out, sem):
    copies = [pltpu.make_async_copy(text, text_out, sem.at[1])]
    for i in range(CHIPS):
        rows = pl.ds(i * (ROWS // CHIPS), ROWS // CHIPS)
        copies.append(pltpu.make_async_copy(video.at[rows, :], video_out.at[rows, :], sem.at[0]))
    for copy in copies:
        copy.start()
    for copy in copies:
        copy.wait()


def on_device(video_query, video_key, video_value, text_query, text_key, text_value, text_length):
    any_spec = pl.BlockSpec(memory_space=pltpu.HBM)
    dma = pltpu.SemaphoreType.DMA
    vmem_spec = pl.BlockSpec(memory_space=pltpu.VMEM)
    width = video_query.shape[1]
    flops = 4 * HEADS_HERE * XS * PAIR * KEYS * HEAD
    out_shape = (
        pltpu.VMEM((ROWS, width), jnp.bfloat16),
        pltpu.VMEM((OUT_TEXT, width), jnp.bfloat16),
    )
    inputs = [
        pltpu.with_memory_space_constraint(a, pltpu.HBM)
        for a in (video_query, video_key, video_value, text_query, text_key, text_value)
    ]
    video, text = pl.pallas_call(
        kernel,
        out_shape=out_shape,
        in_specs=[any_spec] * 7,
        out_specs=(vmem_spec, vmem_spec),
        scratch_shapes=[
            pltpu.VMEM((HEADS_HERE, KEYS, HEAD), jnp.bfloat16),
            pltpu.VMEM((HEADS_HERE, KEYS, 2 * HEAD), jnp.bfloat16),
            pltpu.VMEM((HEADS_HERE, XS * PAIR, HEAD), jnp.bfloat16),
            pltpu.VMEM((HEADS_HERE, XS * PAIR, HEAD), jnp.bfloat16),
            pltpu.VMEM((OUT_TEXT, width), jnp.bfloat16),
            pltpu.SMEM((1,), jnp.int32),
            dma,
            dma,
            dma,
            dma((2, HEADS_HERE)),
            dma((HEADS_HERE, XS)),
            dma((3, HEADS_HERE)),
            dma((2, HEADS_HERE)),
            dma((2, HEADS_HERE)),
            dma,
            dma((HEADS_HERE,)),
            dma,
            dma((HEADS_HERE,)),
        ],
        cost_estimate=pl.CostEstimate(
            flops=flops, bytes_accessed=8 * ROWS * width, transcendentals=flops // (4 * HEAD)
        ),
        compiler_params=pltpu.CompilerParams(
            collective_id=0, has_side_effects=True, vmem_limit_bytes=52 * 2**20
        ),
        name="joint_attention",
    )(text_length, *inputs)
    return pl.pallas_call(
        copy_out,
        out_shape=(
            jax.ShapeDtypeStruct((ROWS, width), jnp.bfloat16),
            jax.ShapeDtypeStruct((OUT_TEXT, width), jnp.bfloat16),
        ),
        in_specs=[vmem_spec] * 2,
        out_specs=(any_spec, any_spec),
        scratch_shapes=[dma((2,))],
        name="copy_out",
    )(*(pltpu.with_memory_space_constraint(a, pltpu.VMEM) for a in (video, text)))


def solution(mesh):
    assert mesh.shape["blk"] == ZS and mesh.shape["ulysses"] == XS * CORES
    tokens = P(("dp", "blk", "ulysses"), None)
    text = P(("dp", "ulysses"), None)
    return jax.shard_map(
        on_device,
        mesh=mesh,
        in_specs=(tokens, tokens, tokens, text, text, text, P("dp")),
        out_specs=(tokens, tokens),
        check_vma=False,
    )
```

```python
import math

import jax
import jax.numpy as jnp
from jax import lax
from jax.experimental import pallas as pl
from jax.experimental.pallas import tpu as pltpu
from jax.sharding import PartitionSpec as P

MESH = pl.DeviceIdType.MESH
HEAD = 128
NEG_BIG = -1e30
SCALE = HEAD ** -0.5 * math.log2(math.e)
XS, ZS, CORES = 4, 2, 2
CHIPS = XS * ZS
HEADS_HERE = 3
ROWS = 256
TEXT_ROWS = 32
OUT_TEXT = 16
KEYS = CORES * (CHIPS * ROWS + XS * TEXT_ROWS)
PAIR = ZS * ROWS + TEXT_ROWS
PEERS = ((1, 0), (3, 0), (2, 0), (0, 1), (1, 1), (3, 1), (2, 1))
QUERY_PEERS = ((3, 0), (3, 1), (2, 0), (2, 1), (1, 0), (1, 1), (0, 1))
PLANE = XS * ROWS
TEXT_HERE = XS * TEXT_ROWS
NEAR = PLANE + TEXT_HERE
VIDEO_1 = CHIPS * ROWS + CORES * TEXT_HERE
BLOCKS = (
    (CHIPS * ROWS, VIDEO_1),
    (0, 1024),
    (1024, 2048),
    (VIDEO_1, VIDEO_1 + 1024),
    (VIDEO_1 + 1024, VIDEO_1 + 2048),
)


def dot(a, b, dims):
    return lax.dot_general(a, b, (dims, ((), ())), preferred_element_type=jnp.float32)


def wait_for(ref, sem):
    pltpu.make_async_copy(ref, ref, sem).wait()


def kernel(
    length_in, vq, vk, vv, tq, tk, tv, vo, to,
    keys, values, queries, outs, staged, length, length_sem, stage_send, stage_recv,
    recv, query_recv, send, sib_recv, sib_send, out_recv, out_send, text_recv, text_send,
):
    u = lax.axis_index("ulysses")
    z = lax.axis_index("blk")
    x, c = u // CORES, lax.rem(u, CORES)

    def device(px, pz, pc):
        return {"blk": pz, "ulysses": px * CORES + pc}

    length_copy = pltpu.make_async_copy(length_in, length, length_sem)
    length_copy.start()

    barrier = pltpu.get_barrier_semaphore()
    for dx, dz in PEERS:
        pl.semaphore_signal(
            barrier,
            inc=1,
            device_id=device(lax.rem(x + dx, XS), lax.rem(z + dz, ZS), c),
            device_id_type=MESH,
        )
    pl.semaphore_signal(barrier, inc=1, device_id=device(x, z, 1 - c), device_id_type=MESH)
    pl.semaphore_wait(barrier, CHIPS)

    def columns(px, pz, h):
        return pl.ds(pl.multiple_of(((px * ZS + pz) * HEADS_HERE + h) * HEAD, HEAD), HEAD)

    key_rows = (
        pl.ds(pl.multiple_of(PLANE + c * (VIDEO_1 - PLANE) + x * ROWS, 16), ROWS),
        pl.ds(pl.multiple_of(c * (VIDEO_1 + PLANE) + x * ROWS, 16), ROWS),
    )
    key_text = pl.ds(pl.multiple_of(CHIPS * ROWS + c * TEXT_HERE + x * TEXT_ROWS, 16), TEXT_ROWS)
    query_rows = tuple(pl.ds(pl.multiple_of(x * PAIR + dz * ROWS, 16), ROWS) for dz in (0, 1))
    own_text = pl.ds(pl.multiple_of(x * PAIR + ZS * ROWS + c * OUT_TEXT, 16), OUT_TEXT)
    other_text = pl.ds(pl.multiple_of(x * PAIR + ZS * ROWS + (1 - c) * OUT_TEXT, 16), OUT_TEXT)

    def key_piece(pc, far):
        if far:
            return pl.ds(pl.multiple_of(pc * (VIDEO_1 + PLANE), 16), PLANE)
        return pl.ds(pl.multiple_of(PLANE + pc * NEAR, 16), NEAR)

    lanes = pl.ds(0, HEAD)

    stage = pltpu.make_async_remote_copy(
        src_ref=tq.at[pl.ds(pl.multiple_of((1 - c) * OUT_TEXT, 16), OUT_TEXT), :],
        dst_ref=staged,
        send_sem=stage_send,
        recv_sem=stage_recv,
        device_id=device(x, z, 1 - c),
        device_id_type=MESH,
    )
    stage.start()

    def scatter(h, pieces, dst, sems, peers, own=True, rows=None):
        for dx, dz in peers:
            px, pz = lax.rem(x + dx, XS), lax.rem(z + dz, ZS)
            pltpu.make_async_remote_copy(
                src_ref=pieces.at[:, columns(px, pz, h)],
                dst_ref=dst if rows is None else dst.at[rows[dz], :],
                send_sem=sems[0],
                recv_sem=sems[1],
                device_id=device(px, pz, c),
                device_id_type=MESH,
            ).start()
        if own:
            place = dst if rows is None else dst.at[rows[0], :]
            pltpu.make_async_copy(pieces.at[:, columns(x, z, h)], place, sems[1]).start()

    near = tuple(p for p in PEERS if p[1] == 0)
    far = tuple(p for p in PEERS if p[1] == 1)
    tq_own = tq.at[pl.ds(pl.multiple_of(c * OUT_TEXT, 16), OUT_TEXT), :]

    def scatter_head(h, carry):
        for i, (video, text, place) in enumerate(((vk, tk, keys), (vv, tv, values))):
            sems = send.at[i, h], recv.at[i, h, 0]
            scatter(h, video, place.at[h, key_rows[0], lanes], sems, near)
            scatter(h, text, place.at[h, key_text, lanes], sems, near)
            sems = send.at[i, h], recv.at[i, h, 1]
            scatter(h, video, place.at[h, key_rows[1], lanes], sems, far, own=False)
        sems = send.at[2, h], query_recv.at[h, x]
        scatter(h, vq, queries.at[h], sems, QUERY_PEERS, rows=query_rows)

        @pl.when(h == 0)
        def _():
            stage.wait()

        scatter(h, tq_own, queries.at[h, own_text, :], sems, near)
        scatter(h, staged, queries.at[h, other_text, :], sems, near)
        return carry

    lax.fori_loop(0, HEADS_HERE, scatter_head, 0)

    for h in range(HEADS_HERE):
        values[h, :, HEAD:] = jnp.ones((KEYS, HEAD), jnp.bfloat16)

    def to_sibling(i, place, h, far):
        rows = key_piece(c, far)
        wait_for(place.at[h, rows, lanes], recv.at[i, h, far])
        pltpu.make_async_remote_copy(
            src_ref=place.at[h, rows, lanes],
            dst_ref=place.at[h, rows, lanes],
            send_sem=sib_send.at[i, h, far],
            recv_sem=sib_recv.at[i, h, far],
            device_id=device(x, z, 1 - c),
            device_id_type=MESH,
        ).start()

    def attend(h, b, first=0, count=PAIR):
        rows = pl.ds(pl.multiple_of(b * PAIR + first, 16), count)
        q = queries[h, rows, :]
        t = lax.broadcasted_iota(jnp.int32, (1, CORES * XS * TEXT_ROWS), 1)
        part = XS * TEXT_ROWS
        position = (
            (lax.rem(t, part) // TEXT_ROWS) * (CORES * TEXT_ROWS)
            + (t // part) * TEXT_ROWS
            + lax.rem(t, TEXT_ROWS)
        )
        valid = position < length[0]
        top = None
        first, last = BLOCKS[0]
        scores = dot(q, keys[h, first:last, :], ((1,), (1,)))
        scores = jnp.where(valid, scores, NEG_BIG)
        for j, (first, last) in enumerate(BLOCKS):
            if j + 1 < len(BLOCKS):
                lo, hi = BLOCKS[j + 1]
                following = dot(q, keys[h, lo:hi, :], ((1,), (1,)))
            here = jnp.max(scores, axis=1, keepdims=True)
            new_top = here if top is None else jnp.maximum(top, here)
            weights = jnp.exp2(scores * SCALE - new_top * SCALE).astype(jnp.bfloat16)
            product = dot(weights, values[h, first:last, :], ((1,), (0,)))
            if top is None:
                summed = product
            else:
                summed = summed * jnp.exp2((top - new_top) * SCALE) + product
            top = new_top
            if j + 1 < len(BLOCKS):
                scores = following
        outs[h, rows, :] = (summed[:, :HEAD] / summed[:, HEAD:]).astype(jnp.bfloat16)

    def video_back(h, b, dz):
        pz = lax.rem(z + dz, ZS)
        return pltpu.make_async_remote_copy(
            src_ref=outs.at[h, pl.ds(pl.multiple_of(b * PAIR + dz * ROWS, 16), ROWS), :],
            dst_ref=vo.at[:, columns(x, z, h)],
            send_sem=out_send.at[h],
            recv_sem=out_recv,
            device_id=device(b, pz, c),
            device_id_type=MESH,
        )

    def text_place(h, b, k):
        src = outs.at[
            h, pl.ds(pl.multiple_of(b * PAIR + ZS * ROWS + k * OUT_TEXT, 16), OUT_TEXT), :
        ]
        px, pz = lax.rem(b, ZS) * CORES + k, b // ZS
        return src, to.at[:, columns(x, z, h)], px, pz, (px == x) & (pz == z)

    def text_back(h, b, k):
        src, dst, px, pz, own = text_place(h, b, k)
        return own, pltpu.make_async_remote_copy(
            src_ref=src,
            dst_ref=dst,
            send_sem=text_send.at[h],
            recv_sem=text_recv,
            device_id=device(px, pz, c),
            device_id_type=MESH,
        )

    length_copy.wait()
    for i, place in ((0, keys), (1, values)):
        for part in range(2):
            to_sibling(i, place, 0, part)

    def near_back(h, i, b):
        @pl.when(i < XS - 1)
        def _():
            video_back(h, b, 0).start()

        @pl.when(i == XS - 1)
        def _():
            pltpu.make_async_copy(
                outs.at[h, query_rows[0], :], vo.at[:, columns(x, z, h)], out_recv
            ).start()

    def far_back(h, b):
        video_back(h, b, 1).start()

        for k in range(CORES):
            own, copy = text_back(h, b, k)
            src, dst, _, _, _ = text_place(h, b, k)

            @pl.when(own)
            def _():
                pltpu.make_async_copy(src, dst, text_recv).start()

            @pl.when(jnp.logical_not(own))
            def _():
                copy.start()

    def give_back(h, i, b):
        far_back(h, b)
        near_back(h, i, b)

    def turn(t, carry):
        h, i = t // XS, lax.rem(t, XS)
        b = lax.rem(x + 1 + i, XS)

        wait_for(
            queries.at[h, pl.ds(pl.multiple_of(b * PAIR, 16), PAIR), :], query_recv.at[h, b]
        )

        @pl.when(i == 0)
        def _():
            for part in range(2):
                rows = key_piece(1 - c, part)
                wait_for(keys.at[h, rows, lanes], sib_recv.at[0, h, part])
                wait_for(values.at[h, rows, lanes], sib_recv.at[1, h, part])

        @pl.when((i == XS - 2) & (h < HEADS_HERE - 1))
        def _():
            to_sibling(0, keys, h + 1, 0)
            to_sibling(0, keys, h + 1, 1)


        last = t == HEADS_HERE * XS - 1

        @pl.when(jnp.logical_not(last))
        def _():
            attend(h, b)

        @pl.when(last)
        def _():
            attend(h, b, ROWS, PAIR - ROWS)
            far_back(h, b)
            attend(h, b, 0, ROWS)
            near_back(h, i, b)

        @pl.when((h == HEADS_HERE - 1) & jnp.logical_not(last))
        def _():
            give_back(h, i, b)

        @pl.when((i == XS - 1) & (h < HEADS_HERE - 1))
        def _():
            to_sibling(1, values, h + 1, 0)
            to_sibling(1, values, h + 1, 1)

        @pl.when((h == HEADS_HERE - 2) & (i == XS - 1))
        def _():
            def early(n, carry):
                ii = lax.rem(n, XS)
                give_back(n // XS, ii, lax.rem(x + 1 + ii, XS))
                return carry

            lax.fori_loop(0, (HEADS_HERE - 1) * XS, early, 0)

        return carry

    lax.fori_loop(0, HEADS_HERE * XS, turn, 0)

    def finish(h, carry):
        for i in range(3):
            sent = (CHIPS - 1) * ROWS + (XS - 1) * TEXT_ROWS
            wait_for(outs.at[h, pl.ds(0, sent), :], send.at[i, h])
        for i, place in ((0, keys), (1, values)):
            for part in range(2):
                wait_for(place.at[h, key_piece(c, part), lanes], sib_send.at[i, h, part])
        wait_for(outs.at[h, pl.ds(0, (CHIPS - 1) * ROWS), :], out_send.at[h])
        for b in range(XS):
            for k in range(CORES):
                own, copy = text_back(h, b, k)

                @pl.when(jnp.logical_not(own))
                def _():
                    copy.wait_send()

        return carry

    lax.fori_loop(0, HEADS_HERE, finish, 0)
    wait_for(vo, out_recv)
    wait_for(to, text_recv)


def copy_out(video, text, video_out, text_out, sem):
    copies = [pltpu.make_async_copy(text, text_out, sem.at[1])]
    for i in range(CHIPS):
        rows = pl.ds(i * (ROWS // CHIPS), ROWS // CHIPS)
        copies.append(pltpu.make_async_copy(video.at[rows, :], video_out.at[rows, :], sem.at[0]))
    for copy in copies:
        copy.start()
    for copy in copies:
        copy.wait()


def on_device(video_query, video_key, video_value, text_query, text_key, text_value, text_length):
    any_spec = pl.BlockSpec(memory_space=pltpu.HBM)
    dma = pltpu.SemaphoreType.DMA
    vmem_spec = pl.BlockSpec(memory_space=pltpu.VMEM)
    width = video_query.shape[1]
    flops = 4 * HEADS_HERE * XS * PAIR * KEYS * HEAD
    out_shape = (
        pltpu.VMEM((ROWS, width), jnp.bfloat16),
        pltpu.VMEM((OUT_TEXT, width), jnp.bfloat16),
    )
    inputs = [
        pltpu.with_memory_space_constraint(a, pltpu.HBM)
        for a in (video_query, video_key, video_value, text_query, text_key, text_value)
    ]
    video, text = pl.pallas_call(
        kernel,
        out_shape=out_shape,
        in_specs=[any_spec] * 7,
        out_specs=(vmem_spec, vmem_spec),
        scratch_shapes=[
            pltpu.VMEM((HEADS_HERE, KEYS, HEAD), jnp.bfloat16),
            pltpu.VMEM((HEADS_HERE, KEYS, 2 * HEAD), jnp.bfloat16),
            pltpu.VMEM((HEADS_HERE, XS * PAIR, HEAD), jnp.bfloat16),
            pltpu.VMEM((HEADS_HERE, XS * PAIR, HEAD), jnp.bfloat16),
            pltpu.VMEM((OUT_TEXT, width), jnp.bfloat16),
            pltpu.SMEM((1,), jnp.int32),
            dma,
            dma,
            dma,
            dma((2, HEADS_HERE, 2)),
            dma((HEADS_HERE, XS)),
            dma((3, HEADS_HERE)),
            dma((2, HEADS_HERE, 2)),
            dma((2, HEADS_HERE, 2)),
            dma,
            dma((HEADS_HERE,)),
            dma,
            dma((HEADS_HERE,)),
        ],
        cost_estimate=pl.CostEstimate(
            flops=flops, bytes_accessed=8 * ROWS * width, transcendentals=flops // (4 * HEAD)
        ),
        compiler_params=pltpu.CompilerParams(
            collective_id=0, has_side_effects=True, vmem_limit_bytes=52 * 2**20
        ),
        name="joint_attention",
    )(text_length, *inputs)
    return pl.pallas_call(
        copy_out,
        out_shape=(
            jax.ShapeDtypeStruct((ROWS, width), jnp.bfloat16),
            jax.ShapeDtypeStruct((OUT_TEXT, width), jnp.bfloat16),
        ),
        in_specs=[vmem_spec] * 2,
        out_specs=(any_spec, any_spec),
        scratch_shapes=[dma((2,))],
        name="copy_out",
    )(*(pltpu.with_memory_space_constraint(a, pltpu.VMEM) for a in (video, text)))


def solution(mesh):
    assert mesh.shape["blk"] == ZS and mesh.shape["ulysses"] == XS * CORES
    tokens = P(("dp", "blk", "ulysses"), None)
    text = P(("dp", "ulysses"), None)
    return jax.shard_map(
        on_device,
        mesh=mesh,
        in_specs=(tokens, tokens, tokens, text, text, text, P("dp")),
        out_specs=(tokens, tokens),
        check_vma=False,
    )
```

```python
import math

import jax
import jax.numpy as jnp
from jax import lax
from jax.experimental import pallas as pl
from jax.experimental.pallas import tpu as pltpu
from jax.sharding import PartitionSpec as P

MESH = pl.DeviceIdType.MESH
HEAD = 128
NEG_BIG = -1e30
SCALE = HEAD ** -0.5 * math.log2(math.e)
XS, ZS, CORES = 4, 2, 2
CHIPS = XS * ZS
HEADS_HERE = 3
ROWS = 256
TEXT_ROWS = 32
OUT_TEXT = 16
KEYS = CORES * CHIPS * ROWS
PAIR = ZS * ROWS + TEXT_ROWS
PEERS = ((1, 0), (3, 0), (2, 0), (0, 1), (1, 1), (3, 1), (2, 1))
QUERY_PEERS = ((3, 0), (3, 1), (2, 0), (2, 1), (1, 0), (1, 1), (0, 1))
PLANE = XS * ROWS
VIDEO_PAIR = ZS * ROWS
TEXT_HERE = XS * TEXT_ROWS
WIDTH = HEADS_HERE * HEAD


def dot(a, b, dims):
    return lax.dot_general(a, b, (dims, ((), ())), preferred_element_type=jnp.float32)


def wait_for(ref, sem):
    pltpu.make_async_copy(ref, ref, sem).wait()


def kernel(
    length_in, vq, vk, vv, tq, tk, tv, vo, to,
    keys, values, queries, outs, text_keys, text_values, text_queries, staged,
    length, length_sem, stage_send, stage_recv, stage_own,
    words_recv, words_send, words_sib_recv, words_sib_send,
    recv, query_recv, send, sib_recv, sib_send, out_recv, out_send, text_recv, text_send,
):
    u = lax.axis_index("ulysses")
    z = lax.axis_index("blk")
    x, c = u // CORES, lax.rem(u, CORES)

    def device(px, pz, pc):
        return {"blk": pz, "ulysses": px * CORES + pc}

    length_copy = pltpu.make_async_copy(length_in, length, length_sem)
    length_copy.start()

    barrier = pltpu.get_barrier_semaphore()
    for dx, dz in PEERS:
        pl.semaphore_signal(
            barrier,
            inc=1,
            device_id=device(lax.rem(x + dx, XS), lax.rem(z + dz, ZS), c),
            device_id_type=MESH,
        )
    pl.semaphore_signal(barrier, inc=1, device_id=device(x, z, 1 - c), device_id_type=MESH)
    pl.semaphore_wait(barrier, CHIPS)

    def columns(px, pz, h):
        return pl.ds(pl.multiple_of(((px * ZS + pz) * HEADS_HERE + h) * HEAD, HEAD), HEAD)

    def word_columns(px, pz):
        return pl.ds(pl.multiple_of((px * ZS + pz) * WIDTH, HEAD), WIDTH)

    key_rows = tuple(
        pl.ds(pl.multiple_of((c * ZS + far) * PLANE + x * ROWS, 16), ROWS) for far in (0, 1)
    )
    key_words = pl.ds(pl.multiple_of(c * TEXT_HERE + x * TEXT_ROWS, 16), TEXT_ROWS)
    words_mine = pl.ds(pl.multiple_of(c * TEXT_HERE, 16), TEXT_HERE)
    words_theirs = pl.ds(pl.multiple_of((1 - c) * TEXT_HERE, 16), TEXT_HERE)
    query_rows = tuple(
        pl.ds(pl.multiple_of(x * VIDEO_PAIR + far * ROWS, 16), ROWS) for far in (0, 1)
    )
    query_words = pl.ds(pl.multiple_of(x * TEXT_ROWS, 16), TEXT_ROWS)

    def key_piece(pc, far):
        return pl.ds(pl.multiple_of((pc * ZS + far) * PLANE, 16), PLANE)

    lanes = pl.ds(0, HEAD)

    def half(k):
        return pl.ds(pl.multiple_of(k * OUT_TEXT, 16), OUT_TEXT)

    stage = pltpu.make_async_remote_copy(
        src_ref=tq.at[half(1 - c), :],
        dst_ref=staged.at[half(c), :],
        send_sem=stage_send,
        recv_sem=stage_recv,
        device_id=device(x, z, 1 - c),
        device_id_type=MESH,
    )
    stage.start()
    stay = pltpu.make_async_copy(tq.at[half(c), :], staged.at[half(c), :], stage_own)
    stay.start()

    def scatter(h, pieces, place, rows, sems, peers):
        for dx, dz in peers:
            px, pz = lax.rem(x + dx, XS), lax.rem(z + dz, ZS)
            pltpu.make_async_remote_copy(
                src_ref=pieces.at[:, columns(px, pz, h)],
                dst_ref=place.at[h, rows[dz], lanes],
                send_sem=sems[0],
                recv_sem=sems[1],
                device_id=device(px, pz, c),
                device_id_type=MESH,
            ).start()

    def stays(h, pieces, place, rows, sem):
        pltpu.make_async_copy(
            pieces.at[:, columns(x, z, h)], place.at[h, rows[0], lanes], sem
        ).start()

    near = tuple(p for p in PEERS if p[1] == 0)
    far = tuple(p for p in PEERS if p[1] == 1)

    def scatter_words(i, pieces, place, rows):
        for dx, _ in near:
            px = lax.rem(x + dx, XS)
            pltpu.make_async_remote_copy(
                src_ref=pieces.at[:, word_columns(px, z)],
                dst_ref=place.at[rows, :],
                send_sem=words_send.at[i],
                recv_sem=words_recv.at[i],
                device_id=device(px, z, c),
                device_id_type=MESH,
            ).start()
        pltpu.make_async_copy(
            pieces.at[:, word_columns(x, z)], place.at[rows, :], words_recv.at[i]
        ).start()

    def scatter_head(h, carry):
        for i, (video, place) in enumerate(((vk, keys), (vv, values))):
            scatter(h, video, place, key_rows, (send.at[i, h], recv.at[i, h, 0]), near)
            scatter(h, video, place, key_rows, (send.at[i, h], recv.at[i, h, 1]), far)
            stays(h, video, place, key_rows, recv.at[i, h, 0])

        @pl.when(h == 0)
        def _():
            scatter_words(0, tk, text_keys, key_words)
            scatter_words(1, tv, text_values, key_words)
            stay.wait()
            stage.wait()
            scatter_words(2, staged, text_queries, query_words)

        sems = send.at[2, h], query_recv.at[h, x]
        scatter(h, vq, queries, query_rows, sems, QUERY_PEERS[:-3])

        @pl.when(x == 0)
        def _():
            scatter(h, vq, queries, query_rows, sems, QUERY_PEERS[-1:] + QUERY_PEERS[-3:-1])

        @pl.when(x > 0)
        def _():
            scatter(h, vq, queries, query_rows, sems, QUERY_PEERS[-3:])

        stays(h, vq, queries, query_rows, query_recv.at[h, x])
        return carry

    lax.fori_loop(0, HEADS_HERE, scatter_head, 0)

    for h in range(HEADS_HERE):
        values[h, :, HEAD:] = jnp.ones((KEYS, HEAD), jnp.bfloat16)

    def to_sibling(i, place, h, far):
        rows = key_piece(c, far)
        wait_for(place.at[h, rows, lanes], recv.at[i, h, far])
        pltpu.make_async_remote_copy(
            src_ref=place.at[h, rows, lanes],
            dst_ref=place.at[h, rows, lanes],
            send_sem=sib_send.at[i, h, far],
            recv_sem=sib_recv.at[i, h, far],
            device_id=device(x, z, 1 - c),
            device_id_type=MESH,
        ).start()

    def words_to_sibling(i, place):
        wait_for(place.at[words_mine, :], words_recv.at[i])
        pltpu.make_async_remote_copy(
            src_ref=place.at[words_mine, :],
            dst_ref=place.at[words_mine, :],
            send_sem=words_sib_send.at[i],
            recv_sem=words_sib_recv.at[i],
            device_id=device(x, z, 1 - c),
            device_id_type=MESH,
        ).start()

    def attend(h, b, first=0, count=PAIR):
        head = pl.ds(pl.multiple_of(h * HEAD, HEAD), HEAD)
        video = min(first + count, VIDEO_PAIR) - first
        q = queries[h, pl.ds(pl.multiple_of(b * VIDEO_PAIR + first, 16), video), :]
        if first + count > VIDEO_PAIR:
            words = text_queries[pl.ds(pl.multiple_of(b * TEXT_ROWS, 16), TEXT_ROWS), head]
            q = jnp.concatenate([q, words], axis=0)
        t = lax.broadcasted_iota(jnp.int32, (1, CORES * TEXT_HERE), 1)
        position = (
            (lax.rem(t, TEXT_HERE) // TEXT_ROWS) * (CORES * TEXT_ROWS)
            + (t // TEXT_HERE) * TEXT_ROWS
            + lax.rem(t, TEXT_ROWS)
        )
        scores = dot(q, text_keys[:, head], ((1,), (1,)))
        scores = jnp.where(position < length[0], scores, NEG_BIG)
        ones = jnp.ones((CORES * TEXT_HERE, HEAD), jnp.bfloat16)
        block = jnp.concatenate([text_values[:, head], ones], axis=1)
        top = None
        for lo in range(0, KEYS + 1, PLANE):
            if lo < KEYS:
                following = dot(q, keys[h, lo : lo + PLANE, :], ((1,), (1,)))
            here = jnp.max(scores, axis=1, keepdims=True)
            new_top = here if top is None else jnp.maximum(top, here)
            weights = jnp.exp2(scores * SCALE - new_top * SCALE).astype(jnp.bfloat16)
            product = dot(weights, block, ((1,), (0,)))
            if top is None:
                summed = product
            else:
                summed = summed * jnp.exp2((top - new_top) * SCALE) + product
            top = new_top
            if lo < KEYS:
                scores, block = following, values[h, lo : lo + PLANE, :]
        rows = pl.ds(pl.multiple_of(b * PAIR + first, 16), count)
        outs[h, rows, :] = (summed[:, :HEAD] / summed[:, HEAD:]).astype(jnp.bfloat16)

    def video_back(h, b, dz):
        pz = lax.rem(z + dz, ZS)
        return pltpu.make_async_remote_copy(
            src_ref=outs.at[h, pl.ds(pl.multiple_of(b * PAIR + dz * ROWS, 16), ROWS), :],
            dst_ref=vo.at[:, columns(x, z, h)],
            send_sem=out_send.at[h],
            recv_sem=out_recv,
            device_id=device(b, pz, c),
            device_id_type=MESH,
        )

    def text_place(h, b, k):
        src = outs.at[
            h, pl.ds(pl.multiple_of(b * PAIR + ZS * ROWS + k * OUT_TEXT, 16), OUT_TEXT), :
        ]
        px, pz = lax.rem(b, ZS) * CORES + k, b // ZS
        return src, to.at[:, columns(x, z, h)], px, pz, (px == x) & (pz == z)

    def text_back(h, b, k):
        src, dst, px, pz, own = text_place(h, b, k)
        return own, pltpu.make_async_remote_copy(
            src_ref=src,
            dst_ref=dst,
            send_sem=text_send.at[h],
            recv_sem=text_recv,
            device_id=device(px, pz, c),
            device_id_type=MESH,
        )

    length_copy.wait()
    for i, place in ((0, keys), (1, values)):
        for part in range(2):
            to_sibling(i, place, 0, part)
    words_to_sibling(0, text_keys)
    words_to_sibling(1, text_values)
    wait_for(text_queries, words_recv.at[2])
    for i, place in ((0, text_keys), (1, text_values)):
        wait_for(place.at[words_theirs, :], words_sib_recv.at[i])

    def near_back(h, b):
        @pl.when(b != x)
        def _():
            video_back(h, b, 0).start()

        @pl.when(b == x)
        def _():
            pltpu.make_async_copy(
                outs.at[h, pl.ds(pl.multiple_of(x * PAIR, 16), ROWS), :],
                vo.at[:, columns(x, z, h)],
                out_recv,
            ).start()

    def far_back(h, b):
        video_back(h, b, 1).start()

        for k in range(CORES):
            own, copy = text_back(h, b, k)
            src, dst, _, _, _ = text_place(h, b, k)

            @pl.when(own)
            def _():
                pltpu.make_async_copy(src, dst, text_recv).start()

            @pl.when(jnp.logical_not(own))
            def _():
                copy.start()

    def give_back(h, b):
        far_back(h, b)
        near_back(h, b)

    def place_of(i):
        late = (x == 0) & (i >= XS - 2)
        return lax.rem(x + 1 + jnp.where(late, 2 * XS - 3 - i, i), XS)

    def turn(t, carry):
        h, i = t // XS, lax.rem(t, XS)
        b = place_of(i)

        wait_for(
            queries.at[h, pl.ds(pl.multiple_of(b * VIDEO_PAIR, 16), VIDEO_PAIR), :], query_recv.at[h, b]
        )

        @pl.when(i == 0)
        def _():
            for part in range(2):
                rows = key_piece(1 - c, part)
                wait_for(keys.at[h, rows, lanes], sib_recv.at[0, h, part])
                wait_for(values.at[h, rows, lanes], sib_recv.at[1, h, part])

        @pl.when((i == XS - 2) & (h < HEADS_HERE - 1))
        def _():
            to_sibling(0, keys, h + 1, 0)
            to_sibling(0, keys, h + 1, 1)


        last = t == HEADS_HERE * XS - 1

        @pl.when(jnp.logical_not(last))
        def _():
            attend(h, b)

        @pl.when(last)
        def _():
            attend(h, b, ROWS, PAIR - ROWS)
            far_back(h, b)
            attend(h, b, 0, ROWS)
            near_back(h, b)

        @pl.when((h == HEADS_HERE - 1) & jnp.logical_not(last))
        def _():
            give_back(h, b)

        @pl.when((i == XS - 1) & (h < HEADS_HERE - 1))
        def _():
            to_sibling(1, values, h + 1, 0)
            to_sibling(1, values, h + 1, 1)

        for done in range(HEADS_HERE - 1):

            @pl.when(t == (HEADS_HERE - 1) * XS - 1 + c * done)
            def _():
                def early(ii, carry):
                    give_back(done, place_of(ii))
                    return carry

                lax.fori_loop(0, XS, early, 0)

        return carry

    lax.fori_loop(0, HEADS_HERE * XS, turn, 0)

    def finish(h, carry):
        for i in range(3):
            wait_for(outs.at[h, pl.ds(0, (CHIPS - 1) * ROWS), :], send.at[i, h])
        for i, place in ((0, keys), (1, values)):
            for part in range(2):
                wait_for(place.at[h, key_piece(c, part), lanes], sib_send.at[i, h, part])
        wait_for(outs.at[h, pl.ds(0, (CHIPS - 1) * ROWS), :], out_send.at[h])
        for b in range(XS):
            for k in range(CORES):
                own, copy = text_back(h, b, k)

                @pl.when(jnp.logical_not(own))
                def _():
                    copy.wait_send()

        return carry

    lax.fori_loop(0, HEADS_HERE, finish, 0)
    for i in range(3):
        wait_for(text_keys.at[pl.ds(0, (XS - 1) * TEXT_ROWS), :], words_send.at[i])
    for i, place in ((0, text_keys), (1, text_values)):
        wait_for(place.at[words_mine, :], words_sib_send.at[i])
    wait_for(vo, out_recv)
    wait_for(to, text_recv)


def copy_out(video, text, video_out, text_out, sem):
    copies = [pltpu.make_async_copy(text, text_out, sem.at[1])]
    for i in range(CHIPS):
        rows = pl.ds(i * (ROWS // CHIPS), ROWS // CHIPS)
        copies.append(pltpu.make_async_copy(video.at[rows, :], video_out.at[rows, :], sem.at[0]))
    for copy in copies:
        copy.start()
    for copy in copies:
        copy.wait()


def on_device(video_query, video_key, video_value, text_query, text_key, text_value, text_length):
    any_spec = pl.BlockSpec(memory_space=pltpu.HBM)
    dma = pltpu.SemaphoreType.DMA
    vmem_spec = pl.BlockSpec(memory_space=pltpu.VMEM)
    width = video_query.shape[1]
    flops = 4 * HEADS_HERE * XS * PAIR * (KEYS + CORES * TEXT_HERE) * HEAD
    out_shape = (
        pltpu.VMEM((ROWS, width), jnp.bfloat16),
        pltpu.VMEM((OUT_TEXT, width), jnp.bfloat16),
    )
    inputs = [
        pltpu.with_memory_space_constraint(a, pltpu.HBM)
        for a in (video_query, video_key, video_value, text_query, text_key, text_value)
    ]
    video, text = pl.pallas_call(
        kernel,
        out_shape=out_shape,
        in_specs=[any_spec] * 7,
        out_specs=(vmem_spec, vmem_spec),
        scratch_shapes=[
            pltpu.VMEM((HEADS_HERE, KEYS, HEAD), jnp.bfloat16),
            pltpu.VMEM((HEADS_HERE, KEYS, 2 * HEAD), jnp.bfloat16),
            pltpu.VMEM((HEADS_HERE, XS * VIDEO_PAIR, HEAD), jnp.bfloat16),
            pltpu.VMEM((HEADS_HERE, XS * PAIR, HEAD), jnp.bfloat16),
            pltpu.VMEM((CORES * TEXT_HERE, WIDTH), jnp.bfloat16),
            pltpu.VMEM((CORES * TEXT_HERE, WIDTH), jnp.bfloat16),
            pltpu.VMEM((TEXT_HERE, WIDTH), jnp.bfloat16),
            pltpu.VMEM((TEXT_ROWS, width), jnp.bfloat16),
            pltpu.SMEM((1,), jnp.int32),
            dma,
            dma,
            dma,
            dma,
            dma((3,)),
            dma((3,)),
            dma((2,)),
            dma((2,)),
            dma((2, HEADS_HERE, 2)),
            dma((HEADS_HERE, XS)),
            dma((3, HEADS_HERE)),
            dma((2, HEADS_HERE, 2)),
            dma((2, HEADS_HERE, 2)),
            dma,
            dma((HEADS_HERE,)),
            dma,
            dma((HEADS_HERE,)),
        ],
        cost_estimate=pl.CostEstimate(
            flops=flops, bytes_accessed=8 * ROWS * width, transcendentals=flops // (4 * HEAD)
        ),
        compiler_params=pltpu.CompilerParams(
            collective_id=0, has_side_effects=True, vmem_limit_bytes=52 * 2**20
        ),
        name="joint_attention",
    )(text_length, *inputs)
    return pl.pallas_call(
        copy_out,
        out_shape=(
            jax.ShapeDtypeStruct((ROWS, width), jnp.bfloat16),
            jax.ShapeDtypeStruct((OUT_TEXT, width), jnp.bfloat16),
        ),
        in_specs=[vmem_spec] * 2,
        out_specs=(any_spec, any_spec),
        scratch_shapes=[dma((2,))],
        name="copy_out",
    )(*(pltpu.with_memory_space_constraint(a, pltpu.VMEM) for a in (video, text)))


def solution(mesh):
    assert mesh.shape["blk"] == ZS and mesh.shape["ulysses"] == XS * CORES
    tokens = P(("dp", "blk", "ulysses"), None)
    text = P(("dp", "ulysses"), None)
    return jax.shard_map(
        on_device,
        mesh=mesh,
        in_specs=(tokens, tokens, tokens, text, text, text, P("dp")),
        out_specs=(tokens, tokens),
        check_vma=False,
    )
```

```python
import math

import jax
import jax.numpy as jnp
from jax import lax
from jax.experimental import pallas as pl
from jax.experimental.pallas import tpu as pltpu
from jax.sharding import PartitionSpec as P

MESH = pl.DeviceIdType.MESH
HEAD = 128
NEG_BIG = -1e30
SCALE = HEAD ** -0.5 * math.log2(math.e)
XS, ZS, CORES = 4, 2, 2
CHIPS = XS * ZS
HEADS_HERE = 3
ROWS = 256
TEXT_ROWS = 32
OUT_TEXT = 16
KEYS = CORES * CHIPS * ROWS
PAIR = ZS * ROWS + TEXT_ROWS
PEERS = ((1, 0), (3, 0), (2, 0), (0, 1), (1, 1), (3, 1), (2, 1))
QUERY_PEERS = ((3, 0), (3, 1), (2, 0), (2, 1), (1, 0), (1, 1), (0, 1))
PLANE = XS * ROWS
VIDEO_PAIR = ZS * ROWS
TEXT_HERE = XS * TEXT_ROWS
WIDTH = HEADS_HERE * HEAD


def dot(a, b, dims):
    return lax.dot_general(a, b, (dims, ((), ())), preferred_element_type=jnp.float32)


def wait_for(ref, sem):
    pltpu.make_async_copy(ref, ref, sem).wait()


def kernel(
    length_in, vq, vk, vv, tq, tk, tv, vo, to,
    keys, values, queries, outs, text_keys, text_values, text_queries, staged,
    length, length_sem, stage_send, stage_recv, stage_own,
    words_recv, words_send, words_sib_recv, words_sib_send,
    recv, query_recv, send, sib_recv, sib_send, out_recv, out_send, text_recv, text_send,
):
    u = lax.axis_index("ulysses")
    z = lax.axis_index("blk")
    x, c = u // CORES, lax.rem(u, CORES)

    def device(px, pz, pc):
        return {"blk": pz, "ulysses": px * CORES + pc}

    length_copy = pltpu.make_async_copy(length_in, length, length_sem)
    length_copy.start()

    barrier = pltpu.get_barrier_semaphore()
    for dx, dz in PEERS:
        pl.semaphore_signal(
            barrier,
            inc=1,
            device_id=device(lax.rem(x + dx, XS), lax.rem(z + dz, ZS), c),
            device_id_type=MESH,
        )
    pl.semaphore_signal(barrier, inc=1, device_id=device(x, z, 1 - c), device_id_type=MESH)
    pl.semaphore_wait(barrier, CHIPS)

    def columns(px, pz, h):
        return pl.ds(pl.multiple_of(((px * ZS + pz) * HEADS_HERE + h) * HEAD, HEAD), HEAD)

    def word_columns(px, pz):
        return pl.ds(pl.multiple_of((px * ZS + pz) * WIDTH, HEAD), WIDTH)

    key_rows = tuple(
        pl.ds(pl.multiple_of((c * ZS + far) * PLANE + x * ROWS, 16), ROWS) for far in (0, 1)
    )
    key_words = pl.ds(pl.multiple_of(c * TEXT_HERE + x * TEXT_ROWS, 16), TEXT_ROWS)
    words_mine = pl.ds(pl.multiple_of(c * TEXT_HERE, 16), TEXT_HERE)
    words_theirs = pl.ds(pl.multiple_of((1 - c) * TEXT_HERE, 16), TEXT_HERE)
    query_rows = tuple(
        pl.ds(pl.multiple_of(x * VIDEO_PAIR + far * ROWS, 16), ROWS) for far in (0, 1)
    )
    query_words = pl.ds(pl.multiple_of(x * TEXT_ROWS, 16), TEXT_ROWS)

    def key_piece(pc, far):
        return pl.ds(pl.multiple_of((pc * ZS + far) * PLANE, 16), PLANE)

    lanes = pl.ds(0, HEAD)

    def half(k):
        return pl.ds(pl.multiple_of(k * OUT_TEXT, 16), OUT_TEXT)

    stage = pltpu.make_async_remote_copy(
        src_ref=tq.at[half(1 - c), :],
        dst_ref=staged.at[half(c), :],
        send_sem=stage_send,
        recv_sem=stage_recv,
        device_id=device(x, z, 1 - c),
        device_id_type=MESH,
    )
    stage.start()
    stay = pltpu.make_async_copy(tq.at[half(c), :], staged.at[half(c), :], stage_own)
    stay.start()

    def scatter(h, pieces, place, rows, sems, peers):
        for (dx, dz), (other, _) in zip(peers, peers[::-1]):
            if all(p[1] == dz for p in peers):
                dx = jnp.where(c == 0, dx, other)
            px, pz = lax.rem(x + dx, XS), lax.rem(z + dz, ZS)
            pltpu.make_async_remote_copy(
                src_ref=pieces.at[:, columns(px, pz, h)],
                dst_ref=place.at[h, rows[dz], lanes],
                send_sem=sems[0],
                recv_sem=sems[1],
                device_id=device(px, pz, c),
                device_id_type=MESH,
            ).start()

    def stays(h, pieces, place, rows, sem):
        pltpu.make_async_copy(
            pieces.at[:, columns(x, z, h)], place.at[h, rows[0], lanes], sem
        ).start()

    near = tuple(p for p in PEERS if p[1] == 0)
    far = tuple(p for p in PEERS if p[1] == 1)

    def scatter_words(i, pieces, place, rows):
        for dx, _ in near:
            px = lax.rem(x + dx, XS)
            pltpu.make_async_remote_copy(
                src_ref=pieces.at[:, word_columns(px, z)],
                dst_ref=place.at[rows, :],
                send_sem=words_send.at[i],
                recv_sem=words_recv.at[i],
                device_id=device(px, z, c),
                device_id_type=MESH,
            ).start()
        pltpu.make_async_copy(
            pieces.at[:, word_columns(x, z)], place.at[rows, :], words_recv.at[i]
        ).start()

    def scatter_head(h, carry):
        for i, (video, place) in enumerate(((vk, keys), (vv, values))):
            scatter(h, video, place, key_rows, (send.at[i, h], recv.at[i, h, 0]), near)
            scatter(h, video, place, key_rows, (send.at[i, h], recv.at[i, h, 1]), far)
            stays(h, video, place, key_rows, recv.at[i, h, 0])

        @pl.when(h == 0)
        def _():
            scatter_words(0, tk, text_keys, key_words)
            scatter_words(1, tv, text_values, key_words)
            stay.wait()
            stage.wait()
            scatter_words(2, staged, text_queries, query_words)

        sems = send.at[2, h], query_recv.at[h, x]
        scatter(h, vq, queries, query_rows, sems, QUERY_PEERS[:-3])

        @pl.when(x == 0)
        def _():
            scatter(h, vq, queries, query_rows, sems, QUERY_PEERS[-1:] + QUERY_PEERS[-3:-1])

        @pl.when(x > 0)
        def _():
            scatter(h, vq, queries, query_rows, sems, QUERY_PEERS[-3:])

        stays(h, vq, queries, query_rows, query_recv.at[h, x])
        return carry

    lax.fori_loop(0, HEADS_HERE, scatter_head, 0)

    for h in range(HEADS_HERE):
        values[h, :, HEAD:] = jnp.ones((KEYS, HEAD), jnp.bfloat16)

    def to_sibling(i, place, h, far):
        rows = key_piece(c, far)
        wait_for(place.at[h, rows, lanes], recv.at[i, h, far])
        pltpu.make_async_remote_copy(
            src_ref=place.at[h, rows, lanes],
            dst_ref=place.at[h, rows, lanes],
            send_sem=sib_send.at[i, h, far],
            recv_sem=sib_recv.at[i, h, far],
            device_id=device(x, z, 1 - c),
            device_id_type=MESH,
        ).start()

    def words_to_sibling(i, place):
        wait_for(place.at[words_mine, :], words_recv.at[i])
        pltpu.make_async_remote_copy(
            src_ref=place.at[words_mine, :],
            dst_ref=place.at[words_mine, :],
            send_sem=words_sib_send.at[i],
            recv_sem=words_sib_recv.at[i],
            device_id=device(x, z, 1 - c),
            device_id_type=MESH,
        ).start()

    def attend(h, b, first=0, count=PAIR):
        head = pl.ds(pl.multiple_of(h * HEAD, HEAD), HEAD)
        video = min(first + count, VIDEO_PAIR) - first
        q = queries[h, pl.ds(pl.multiple_of(b * VIDEO_PAIR + first, 16), video), :]
        if first + count > VIDEO_PAIR:
            words = text_queries[pl.ds(pl.multiple_of(b * TEXT_ROWS, 16), TEXT_ROWS), head]
            q = jnp.concatenate([q, words], axis=0)
        t = lax.broadcasted_iota(jnp.int32, (1, CORES * TEXT_HERE), 1)
        position = (
            (lax.rem(t, TEXT_HERE) // TEXT_ROWS) * (CORES * TEXT_ROWS)
            + (t // TEXT_HERE) * TEXT_ROWS
            + lax.rem(t, TEXT_ROWS)
        )
        scores = dot(q, text_keys[:, head], ((1,), (1,)))
        scores = jnp.where(position < length[0], scores, NEG_BIG)
        ones = jnp.ones((CORES * TEXT_HERE, HEAD), jnp.bfloat16)
        block = jnp.concatenate([text_values[:, head], ones], axis=1)
        top = None
        for lo in range(0, KEYS + 1, PLANE):
            if lo < KEYS:
                following = dot(q, keys[h, lo : lo + PLANE, :], ((1,), (1,)))
            here = jnp.max(scores, axis=1, keepdims=True)
            new_top = here if top is None else jnp.maximum(top, here)
            weights = jnp.exp2(scores * SCALE - new_top * SCALE).astype(jnp.bfloat16)
            product = dot(weights, block, ((1,), (0,)))
            if top is None:
                summed = product
            else:
                summed = summed * jnp.exp2((top - new_top) * SCALE) + product
            top = new_top
            if lo < KEYS:
                scores, block = following, values[h, lo : lo + PLANE, :]
        rows = pl.ds(pl.multiple_of(b * PAIR + first, 16), count)
        outs[h, rows, :] = (summed[:, :HEAD] / summed[:, HEAD:]).astype(jnp.bfloat16)

    def video_back(h, b, dz):
        pz = lax.rem(z + dz, ZS)
        return pltpu.make_async_remote_copy(
            src_ref=outs.at[h, pl.ds(pl.multiple_of(b * PAIR + dz * ROWS, 16), ROWS), :],
            dst_ref=vo.at[:, columns(x, z, h)],
            send_sem=out_send.at[h],
            recv_sem=out_recv,
            device_id=device(b, pz, c),
            device_id_type=MESH,
        )

    def text_place(h, b, k):
        src = outs.at[
            h, pl.ds(pl.multiple_of(b * PAIR + ZS * ROWS + k * OUT_TEXT, 16), OUT_TEXT), :
        ]
        px, pz = lax.rem(b, ZS) * CORES + k, b // ZS
        return src, to.at[:, columns(x, z, h)], px, pz, (px == x) & (pz == z)

    def text_back(h, b, k):
        src, dst, px, pz, own = text_place(h, b, k)
        return own, pltpu.make_async_remote_copy(
            src_ref=src,
            dst_ref=dst,
            send_sem=text_send.at[h],
            recv_sem=text_recv,
            device_id=device(px, pz, c),
            device_id_type=MESH,
        )

    length_copy.wait()
    for i, place in ((0, keys), (1, values)):
        for part in range(2):
            to_sibling(i, place, 0, part)
    words_to_sibling(0, text_keys)
    words_to_sibling(1, text_values)
    wait_for(text_queries, words_recv.at[2])
    for i, place in ((0, text_keys), (1, text_values)):
        wait_for(place.at[words_theirs, :], words_sib_recv.at[i])

    def near_back(h, b):
        @pl.when(b != x)
        def _():
            video_back(h, b, 0).start()

        @pl.when(b == x)
        def _():
            pltpu.make_async_copy(
                outs.at[h, pl.ds(pl.multiple_of(x * PAIR, 16), ROWS), :],
                vo.at[:, columns(x, z, h)],
                out_recv,
            ).start()

    def far_back(h, b):
        video_back(h, b, 1).start()

        for k in range(CORES):
            own, copy = text_back(h, b, k)
            src, dst, _, _, _ = text_place(h, b, k)

            @pl.when(own)
            def _():
                pltpu.make_async_copy(src, dst, text_recv).start()

            @pl.when(jnp.logical_not(own))
            def _():
                copy.start()

    def give_back(h, b):
        far_back(h, b)
        near_back(h, b)

    def place_of(i):
        late = (x == 0) & (i >= XS - 2)
        return lax.rem(x + 1 + jnp.where(late, 2 * XS - 3 - i, i), XS)

    def turn(t, carry):
        h, i = t // XS, lax.rem(t, XS)
        b = place_of(i)

        wait_for(
            queries.at[h, pl.ds(pl.multiple_of(b * VIDEO_PAIR, 16), VIDEO_PAIR), :], query_recv.at[h, b]
        )

        @pl.when(i == 0)
        def _():
            for part in range(2):
                rows = key_piece(1 - c, part)
                wait_for(keys.at[h, rows, lanes], sib_recv.at[0, h, part])
                wait_for(values.at[h, rows, lanes], sib_recv.at[1, h, part])

        @pl.when((i == XS - 2) & (h < HEADS_HERE - 1))
        def _():
            to_sibling(0, keys, h + 1, 0)
            to_sibling(0, keys, h + 1, 1)


        last = t == HEADS_HERE * XS - 1

        @pl.when(jnp.logical_not(last))
        def _():
            attend(h, b)

        @pl.when(last)
        def _():
            attend(h, b, ROWS, PAIR - ROWS)
            far_back(h, b)
            attend(h, b, 0, ROWS)
            near_back(h, b)

        @pl.when((h == HEADS_HERE - 1) & jnp.logical_not(last))
        def _():
            give_back(h, b)

        @pl.when((i == XS - 1) & (h < HEADS_HERE - 1))
        def _():
            to_sibling(1, values, h + 1, 0)
            to_sibling(1, values, h + 1, 1)

        for done in range(HEADS_HERE - 1):

            @pl.when(t == (HEADS_HERE - 1) * XS - 1 + c * done)
            def _():
                def early(ii, carry):
                    give_back(done, place_of(ii))
                    return carry

                lax.fori_loop(0, XS, early, 0)

        return carry

    lax.fori_loop(0, HEADS_HERE * XS, turn, 0)

    def finish(h, carry):
        for i in range(3):
            wait_for(outs.at[h, pl.ds(0, (CHIPS - 1) * ROWS), :], send.at[i, h])
        for i, place in ((0, keys), (1, values)):
            for part in range(2):
                wait_for(place.at[h, key_piece(c, part), lanes], sib_send.at[i, h, part])
        wait_for(outs.at[h, pl.ds(0, (CHIPS - 1) * ROWS), :], out_send.at[h])
        for b in range(XS):
            for k in range(CORES):
                own, copy = text_back(h, b, k)

                @pl.when(jnp.logical_not(own))
                def _():
                    copy.wait_send()

        return carry

    lax.fori_loop(0, HEADS_HERE, finish, 0)
    for i in range(3):
        wait_for(text_keys.at[pl.ds(0, (XS - 1) * TEXT_ROWS), :], words_send.at[i])
    for i, place in ((0, text_keys), (1, text_values)):
        wait_for(place.at[words_mine, :], words_sib_send.at[i])
    wait_for(vo, out_recv)
    wait_for(to, text_recv)


def copy_out(video, text, video_out, text_out, sem):
    copies = [pltpu.make_async_copy(text, text_out, sem.at[1])]
    for i in range(CHIPS):
        rows = pl.ds(i * (ROWS // CHIPS), ROWS // CHIPS)
        copies.append(pltpu.make_async_copy(video.at[rows, :], video_out.at[rows, :], sem.at[0]))
    for copy in copies:
        copy.start()
    for copy in copies:
        copy.wait()


def on_device(video_query, video_key, video_value, text_query, text_key, text_value, text_length):
    any_spec = pl.BlockSpec(memory_space=pltpu.HBM)
    dma = pltpu.SemaphoreType.DMA
    vmem_spec = pl.BlockSpec(memory_space=pltpu.VMEM)
    width = video_query.shape[1]
    flops = 4 * HEADS_HERE * XS * PAIR * (KEYS + CORES * TEXT_HERE) * HEAD
    out_shape = (
        pltpu.VMEM((ROWS, width), jnp.bfloat16),
        pltpu.VMEM((OUT_TEXT, width), jnp.bfloat16),
    )
    inputs = [
        pltpu.with_memory_space_constraint(a, pltpu.HBM)
        for a in (video_query, video_key, video_value, text_query, text_key, text_value)
    ]
    video, text = pl.pallas_call(
        kernel,
        out_shape=out_shape,
        in_specs=[any_spec] * 7,
        out_specs=(vmem_spec, vmem_spec),
        scratch_shapes=[
            pltpu.VMEM((HEADS_HERE, KEYS, HEAD), jnp.bfloat16),
            pltpu.VMEM((HEADS_HERE, KEYS, 2 * HEAD), jnp.bfloat16),
            pltpu.VMEM((HEADS_HERE, XS * VIDEO_PAIR, HEAD), jnp.bfloat16),
            pltpu.VMEM((HEADS_HERE, XS * PAIR, HEAD), jnp.bfloat16),
            pltpu.VMEM((CORES * TEXT_HERE, WIDTH), jnp.bfloat16),
            pltpu.VMEM((CORES * TEXT_HERE, WIDTH), jnp.bfloat16),
            pltpu.VMEM((TEXT_HERE, WIDTH), jnp.bfloat16),
            pltpu.VMEM((TEXT_ROWS, width), jnp.bfloat16),
            pltpu.SMEM((1,), jnp.int32),
            dma,
            dma,
            dma,
            dma,
            dma((3,)),
            dma((3,)),
            dma((2,)),
            dma((2,)),
            dma((2, HEADS_HERE, 2)),
            dma((HEADS_HERE, XS)),
            dma((3, HEADS_HERE)),
            dma((2, HEADS_HERE, 2)),
            dma((2, HEADS_HERE, 2)),
            dma,
            dma((HEADS_HERE,)),
            dma,
            dma((HEADS_HERE,)),
        ],
        cost_estimate=pl.CostEstimate(
            flops=flops, bytes_accessed=8 * ROWS * width, transcendentals=flops // (4 * HEAD)
        ),
        compiler_params=pltpu.CompilerParams(
            collective_id=0, has_side_effects=True, vmem_limit_bytes=52 * 2**20
        ),
        name="joint_attention",
    )(text_length, *inputs)
    return pl.pallas_call(
        copy_out,
        out_shape=(
            jax.ShapeDtypeStruct((ROWS, width), jnp.bfloat16),
            jax.ShapeDtypeStruct((OUT_TEXT, width), jnp.bfloat16),
        ),
        in_specs=[vmem_spec] * 2,
        out_specs=(any_spec, any_spec),
        scratch_shapes=[dma((2,))],
        name="copy_out",
    )(*(pltpu.with_memory_space_constraint(a, pltpu.VMEM) for a in (video, text)))


def solution(mesh):
    assert mesh.shape["blk"] == ZS and mesh.shape["ulysses"] == XS * CORES
    tokens = P(("dp", "blk", "ulysses"), None)
    text = P(("dp", "ulysses"), None)
    return jax.shard_map(
        on_device,
        mesh=mesh,
        in_specs=(tokens, tokens, tokens, text, text, text, P("dp")),
        out_specs=(tokens, tokens),
        check_vma=False,
    )
```

```python
import math

import jax
import jax.numpy as jnp
from jax import lax
from jax.experimental import pallas as pl
from jax.experimental.pallas import tpu as pltpu
from jax.sharding import PartitionSpec as P

MESH = pl.DeviceIdType.MESH
HEAD = 128
NEG_BIG = -1e30
SCALE = HEAD ** -0.5 * math.log2(math.e)
XS, ZS, CORES = 4, 2, 2
CHIPS = XS * ZS
HEADS_HERE = 3
ROWS = 256
TEXT_ROWS = 32
OUT_TEXT = 16
KEYS = CORES * CHIPS * ROWS
PAIR = ZS * ROWS + TEXT_ROWS
PEERS = ((1, 0), (3, 0), (2, 0), (0, 1), (1, 1), (3, 1), (2, 1))
QUERY_PEERS = ((3, 0), (3, 1), (2, 0), (2, 1), (1, 0), (1, 1), (0, 1))
PLANE = XS * ROWS
VIDEO_PAIR = ZS * ROWS
TEXT_HERE = XS * TEXT_ROWS
WIDTH = HEADS_HERE * HEAD


def dot(a, b, dims):
    return lax.dot_general(a, b, (dims, ((), ())), preferred_element_type=jnp.float32)


def wait_for(ref, sem):
    pltpu.make_async_copy(ref, ref, sem).wait()


def kernel(
    length_in, vq, vk, vv, tq, tk, tv, vo, to,
    keys, values, queries, outs, text_keys, text_values, text_queries, staged,
    length, length_sem, stage_send, stage_recv, stage_own,
    words_recv, words_send, words_sib_recv, words_sib_send,
    recv, query_recv, send, sib_recv, sib_send, out_recv, out_send, text_recv, text_send,
):
    u = lax.axis_index("ulysses")
    z = lax.axis_index("blk")
    x, c = u // CORES, lax.rem(u, CORES)

    def device(px, pz, pc):
        return {"blk": pz, "ulysses": px * CORES + pc}

    length_copy = pltpu.make_async_copy(length_in, length, length_sem)
    length_copy.start()

    barrier = pltpu.get_barrier_semaphore()
    for dx, dz in PEERS:
        pl.semaphore_signal(
            barrier,
            inc=1,
            device_id=device(lax.rem(x + dx, XS), lax.rem(z + dz, ZS), c),
            device_id_type=MESH,
        )
    pl.semaphore_signal(barrier, inc=1, device_id=device(x, z, 1 - c), device_id_type=MESH)
    pl.semaphore_wait(barrier, CHIPS)

    def columns(px, pz, h):
        return pl.ds(pl.multiple_of(((px * ZS + pz) * HEADS_HERE + h) * HEAD, HEAD), HEAD)

    def word_columns(px, pz):
        return pl.ds(pl.multiple_of((px * ZS + pz) * WIDTH, HEAD), WIDTH)

    key_rows = tuple(
        pl.ds(pl.multiple_of((c * ZS + far) * PLANE + x * ROWS, 16), ROWS) for far in (0, 1)
    )
    key_words = pl.ds(pl.multiple_of(c * TEXT_HERE + x * TEXT_ROWS, 16), TEXT_ROWS)
    words_mine = pl.ds(pl.multiple_of(c * TEXT_HERE, 16), TEXT_HERE)
    words_theirs = pl.ds(pl.multiple_of((1 - c) * TEXT_HERE, 16), TEXT_HERE)
    query_rows = tuple(
        pl.ds(pl.multiple_of(x * VIDEO_PAIR + far * ROWS, 16), ROWS) for far in (0, 1)
    )
    query_words = pl.ds(pl.multiple_of(x * TEXT_ROWS, 16), TEXT_ROWS)

    def key_piece(pc, far):
        return pl.ds(pl.multiple_of((pc * ZS + far) * PLANE, 16), PLANE)

    lanes = pl.ds(0, HEAD)

    def half(k):
        return pl.ds(pl.multiple_of(k * OUT_TEXT, 16), OUT_TEXT)

    stage = pltpu.make_async_remote_copy(
        src_ref=tq.at[half(1 - c), :],
        dst_ref=staged.at[half(c), :],
        send_sem=stage_send,
        recv_sem=stage_recv,
        device_id=device(x, z, 1 - c),
        device_id_type=MESH,
    )
    stage.start()
    stay = pltpu.make_async_copy(tq.at[half(c), :], staged.at[half(c), :], stage_own)
    stay.start()

    def scatter(h, pieces, place, rows, sems, peers):
        for dx, dz in peers:
            px, pz = lax.rem(x + dx, XS), lax.rem(z + dz, ZS)
            pltpu.make_async_remote_copy(
                src_ref=pieces.at[:, columns(px, pz, h)],
                dst_ref=place.at[h, rows[dz], lanes],
                send_sem=sems[0],
                recv_sem=sems[1],
                device_id=device(px, pz, c),
                device_id_type=MESH,
            ).start()

    def stays(h, pieces, place, rows, sem):
        pltpu.make_async_copy(
            pieces.at[:, columns(x, z, h)], place.at[h, rows[0], lanes], sem
        ).start()

    near = tuple(p for p in PEERS if p[1] == 0)
    far = tuple(p for p in PEERS if p[1] == 1)

    def scatter_words(i, pieces, place, rows):
        for dx, _ in near:
            px = lax.rem(x + dx, XS)
            pltpu.make_async_remote_copy(
                src_ref=pieces.at[:, word_columns(px, z)],
                dst_ref=place.at[rows, :],
                send_sem=words_send.at[i],
                recv_sem=words_recv.at[i],
                device_id=device(px, z, c),
                device_id_type=MESH,
            ).start()
        pltpu.make_async_copy(
            pieces.at[:, word_columns(x, z)], place.at[rows, :], words_recv.at[i]
        ).start()

    def scatter_head(h, carry):
        for i, (video, place) in enumerate(((vk, keys), (vv, values))):
            scatter(h, video, place, key_rows, (send.at[i, h], recv.at[i, h, 0]), near)
            scatter(h, video, place, key_rows, (send.at[i, h], recv.at[i, h, 1]), far)
            stays(h, video, place, key_rows, recv.at[i, h, 0])

        @pl.when(h == 0)
        def _():
            scatter_words(0, tk, text_keys, key_words)
            scatter_words(1, tv, text_values, key_words)
            stay.wait()
            stage.wait()
            scatter_words(2, staged, text_queries, query_words)

        sems = send.at[2, h], query_recv.at[h, x]
        scatter(h, vq, queries, query_rows, sems, QUERY_PEERS[:-3])

        @pl.when(x == 0)
        def _():
            scatter(h, vq, queries, query_rows, sems, QUERY_PEERS[-1:] + QUERY_PEERS[-3:-1])

        @pl.when(x > 0)
        def _():
            scatter(h, vq, queries, query_rows, sems, QUERY_PEERS[-3:])

        stays(h, vq, queries, query_rows, query_recv.at[h, x])
        return carry

    lax.fori_loop(0, HEADS_HERE, scatter_head, 0)

    for h in range(HEADS_HERE):
        values[h, :, HEAD:] = jnp.ones((KEYS, HEAD), jnp.bfloat16)

    def to_sibling(i, place, h, far):
        rows = key_piece(c, far)
        wait_for(place.at[h, rows, lanes], recv.at[i, h, far])
        pltpu.make_async_remote_copy(
            src_ref=place.at[h, rows, lanes],
            dst_ref=place.at[h, rows, lanes],
            send_sem=sib_send.at[i, h, far],
            recv_sem=sib_recv.at[i, h, far],
            device_id=device(x, z, 1 - c),
            device_id_type=MESH,
        ).start()

    def words_to_sibling(i, place):
        wait_for(place.at[words_mine, :], words_recv.at[i])
        pltpu.make_async_remote_copy(
            src_ref=place.at[words_mine, :],
            dst_ref=place.at[words_mine, :],
            send_sem=words_sib_send.at[i],
            recv_sem=words_sib_recv.at[i],
            device_id=device(x, z, 1 - c),
            device_id_type=MESH,
        ).start()

    def attend(h, b, first=0, count=PAIR):
        head = pl.ds(pl.multiple_of(h * HEAD, HEAD), HEAD)
        video = min(first + count, VIDEO_PAIR) - first
        q = queries[h, pl.ds(pl.multiple_of(b * VIDEO_PAIR + first, 16), video), :]
        if first + count > VIDEO_PAIR:
            words = text_queries[pl.ds(pl.multiple_of(b * TEXT_ROWS, 16), TEXT_ROWS), head]
            q = jnp.concatenate([q, words], axis=0)
        scaled = q.astype(jnp.float32) * SCALE
        high = scaled.astype(jnp.bfloat16)
        low = (scaled - high.astype(jnp.float32)).astype(jnp.bfloat16)
        q = jnp.concatenate([high, low], axis=1)
        t = lax.broadcasted_iota(jnp.int32, (1, CORES * TEXT_HERE), 1)
        position = (
            (lax.rem(t, TEXT_HERE) // TEXT_ROWS) * (CORES * TEXT_ROWS)
            + (t // TEXT_HERE) * TEXT_ROWS
            + lax.rem(t, TEXT_ROWS)
        )
        words = text_keys[:, head]
        scores = dot(q, jnp.concatenate([words, words], axis=1), ((1,), (1,)))
        scores = jnp.where(position < length[0], scores, NEG_BIG)
        ones = jnp.ones((CORES * TEXT_HERE, HEAD), jnp.bfloat16)
        block = jnp.concatenate([text_values[:, head], ones], axis=1)
        top = None
        for lo in range(0, KEYS + 1, PLANE):
            if lo < KEYS:
                following = dot(q, keys[h, lo : lo + PLANE, :], ((1,), (1,)))
            here = jnp.max(scores, axis=1, keepdims=True)
            new_top = here if top is None else jnp.maximum(top, here)
            weights = jnp.exp2(scores - new_top).astype(jnp.bfloat16)
            product = dot(weights, block, ((1,), (0,)))
            if top is None:
                summed = product
            else:
                summed = summed * jnp.exp2(top - new_top) + product
            top = new_top
            if lo < KEYS:
                scores, block = following, values[h, lo : lo + PLANE, :]
        rows = pl.ds(pl.multiple_of(b * PAIR + first, 16), count)
        outs[h, rows, :] = (summed[:, :HEAD] / summed[:, HEAD:]).astype(jnp.bfloat16)

    def video_back(h, b, dz):
        pz = lax.rem(z + dz, ZS)
        return pltpu.make_async_remote_copy(
            src_ref=outs.at[h, pl.ds(pl.multiple_of(b * PAIR + dz * ROWS, 16), ROWS), :],
            dst_ref=vo.at[:, columns(x, z, h)],
            send_sem=out_send.at[h],
            recv_sem=out_recv,
            device_id=device(b, pz, c),
            device_id_type=MESH,
        )

    def text_place(h, b, k):
        src = outs.at[
            h, pl.ds(pl.multiple_of(b * PAIR + ZS * ROWS + k * OUT_TEXT, 16), OUT_TEXT), :
        ]
        px, pz = lax.rem(b, ZS) * CORES + k, b // ZS
        return src, to.at[:, columns(x, z, h)], px, pz, (px == x) & (pz == z)

    def text_back(h, b, k):
        src, dst, px, pz, own = text_place(h, b, k)
        return own, pltpu.make_async_remote_copy(
            src_ref=src,
            dst_ref=dst,
            send_sem=text_send.at[h],
            recv_sem=text_recv,
            device_id=device(px, pz, c),
            device_id_type=MESH,
        )

    length_copy.wait()
    for i, place in ((0, keys), (1, values)):
        for part in range(2):
            to_sibling(i, place, 0, part)
    words_to_sibling(0, text_keys)
    words_to_sibling(1, text_values)
    wait_for(text_queries, words_recv.at[2])
    for i, place in ((0, text_keys), (1, text_values)):
        wait_for(place.at[words_theirs, :], words_sib_recv.at[i])

    def near_back(h, b):
        @pl.when(b != x)
        def _():
            video_back(h, b, 0).start()

        @pl.when(b == x)
        def _():
            pltpu.make_async_copy(
                outs.at[h, pl.ds(pl.multiple_of(x * PAIR, 16), ROWS), :],
                vo.at[:, columns(x, z, h)],
                out_recv,
            ).start()

    def far_back(h, b):
        video_back(h, b, 1).start()

        for k in range(CORES):
            own, copy = text_back(h, b, k)
            src, dst, _, _, _ = text_place(h, b, k)

            @pl.when(own)
            def _():
                pltpu.make_async_copy(src, dst, text_recv).start()

            @pl.when(jnp.logical_not(own))
            def _():
                copy.start()

    def give_back(h, b):
        far_back(h, b)
        near_back(h, b)

    def place_of(i):
        late = (x == 0) & (i >= XS - 2)
        return lax.rem(x + 1 + jnp.where(late, 2 * XS - 3 - i, i), XS)

    def turn(t, carry):
        h, i = t // XS, lax.rem(t, XS)
        b = place_of(i)

        wait_for(
            queries.at[h, pl.ds(pl.multiple_of(b * VIDEO_PAIR, 16), VIDEO_PAIR), :], query_recv.at[h, b]
        )

        @pl.when(i == 0)
        def _():
            for part in range(2):
                rows = key_piece(1 - c, part)
                wait_for(keys.at[h, rows, lanes], sib_recv.at[0, h, part])
                wait_for(values.at[h, rows, lanes], sib_recv.at[1, h, part])
            keys[h, :, HEAD:] = keys[h, :, :HEAD]

        @pl.when((i == XS - 2) & (h < HEADS_HERE - 1))
        def _():
            to_sibling(0, keys, h + 1, 0)
            to_sibling(0, keys, h + 1, 1)


        last = t == HEADS_HERE * XS - 1

        @pl.when(jnp.logical_not(last))
        def _():
            attend(h, b)

        @pl.when(last)
        def _():
            attend(h, b, ROWS, PAIR - ROWS)
            far_back(h, b)
            attend(h, b, 0, ROWS)
            near_back(h, b)

        @pl.when((h == HEADS_HERE - 1) & jnp.logical_not(last))
        def _():
            give_back(h, b)

        @pl.when((i == XS - 1) & (h < HEADS_HERE - 1))
        def _():
            to_sibling(1, values, h + 1, 0)
            to_sibling(1, values, h + 1, 1)

        for done in range(HEADS_HERE - 1):

            @pl.when(t == (HEADS_HERE - 1) * XS - 1 + c * done)
            def _():
                def early(ii, carry):
                    give_back(done, place_of(ii))
                    return carry

                lax.fori_loop(0, XS, early, 0)

        return carry

    lax.fori_loop(0, HEADS_HERE * XS, turn, 0)

    def finish(h, carry):
        for i in range(3):
            wait_for(outs.at[h, pl.ds(0, (CHIPS - 1) * ROWS), :], send.at[i, h])
        for i, place in ((0, keys), (1, values)):
            for part in range(2):
                wait_for(place.at[h, key_piece(c, part), lanes], sib_send.at[i, h, part])
        wait_for(outs.at[h, pl.ds(0, (CHIPS - 1) * ROWS), :], out_send.at[h])
        for b in range(XS):
            for k in range(CORES):
                own, copy = text_back(h, b, k)

                @pl.when(jnp.logical_not(own))
                def _():
                    copy.wait_send()

        return carry

    lax.fori_loop(0, HEADS_HERE, finish, 0)
    for i in range(3):
        wait_for(text_keys.at[pl.ds(0, (XS - 1) * TEXT_ROWS), :], words_send.at[i])
    for i, place in ((0, text_keys), (1, text_values)):
        wait_for(place.at[words_mine, :], words_sib_send.at[i])
    wait_for(vo, out_recv)
    wait_for(to, text_recv)


def copy_out(video, text, video_out, text_out, sem):
    copies = [pltpu.make_async_copy(text, text_out, sem.at[1])]
    for i in range(CHIPS):
        rows = pl.ds(i * (ROWS // CHIPS), ROWS // CHIPS)
        copies.append(pltpu.make_async_copy(video.at[rows, :], video_out.at[rows, :], sem.at[0]))
    for copy in copies:
        copy.start()
    for copy in copies:
        copy.wait()


def on_device(video_query, video_key, video_value, text_query, text_key, text_value, text_length):
    any_spec = pl.BlockSpec(memory_space=pltpu.HBM)
    dma = pltpu.SemaphoreType.DMA
    vmem_spec = pl.BlockSpec(memory_space=pltpu.VMEM)
    width = video_query.shape[1]
    flops = 4 * HEADS_HERE * XS * PAIR * (KEYS + CORES * TEXT_HERE) * HEAD
    out_shape = (
        pltpu.VMEM((ROWS, width), jnp.bfloat16),
        pltpu.VMEM((OUT_TEXT, width), jnp.bfloat16),
    )
    inputs = [
        pltpu.with_memory_space_constraint(a, pltpu.HBM)
        for a in (video_query, video_key, video_value, text_query, text_key, text_value)
    ]
    video, text = pl.pallas_call(
        kernel,
        out_shape=out_shape,
        in_specs=[any_spec] * 7,
        out_specs=(vmem_spec, vmem_spec),
        scratch_shapes=[
            pltpu.VMEM((HEADS_HERE, KEYS, 2 * HEAD), jnp.bfloat16),
            pltpu.VMEM((HEADS_HERE, KEYS, 2 * HEAD), jnp.bfloat16),
            pltpu.VMEM((HEADS_HERE, XS * VIDEO_PAIR, HEAD), jnp.bfloat16),
            pltpu.VMEM((HEADS_HERE, XS * PAIR, HEAD), jnp.bfloat16),
            pltpu.VMEM((CORES * TEXT_HERE, WIDTH), jnp.bfloat16),
            pltpu.VMEM((CORES * TEXT_HERE, WIDTH), jnp.bfloat16),
            pltpu.VMEM((TEXT_HERE, WIDTH), jnp.bfloat16),
            pltpu.VMEM((TEXT_ROWS, width), jnp.bfloat16),
            pltpu.SMEM((1,), jnp.int32),
            dma,
            dma,
            dma,
            dma,
            dma((3,)),
            dma((3,)),
            dma((2,)),
            dma((2,)),
            dma((2, HEADS_HERE, 2)),
            dma((HEADS_HERE, XS)),
            dma((3, HEADS_HERE)),
            dma((2, HEADS_HERE, 2)),
            dma((2, HEADS_HERE, 2)),
            dma,
            dma((HEADS_HERE,)),
            dma,
            dma((HEADS_HERE,)),
        ],
        cost_estimate=pl.CostEstimate(
            flops=flops, bytes_accessed=8 * ROWS * width, transcendentals=flops // (4 * HEAD)
        ),
        compiler_params=pltpu.CompilerParams(
            collective_id=0, has_side_effects=True, vmem_limit_bytes=52 * 2**20
        ),
        name="joint_attention",
    )(text_length, *inputs)
    return pl.pallas_call(
        copy_out,
        out_shape=(
            jax.ShapeDtypeStruct((ROWS, width), jnp.bfloat16),
            jax.ShapeDtypeStruct((OUT_TEXT, width), jnp.bfloat16),
        ),
        in_specs=[vmem_spec] * 2,
        out_specs=(any_spec, any_spec),
        scratch_shapes=[dma((2,))],
        name="copy_out",
    )(*(pltpu.with_memory_space_constraint(a, pltpu.VMEM) for a in (video, text)))


def solution(mesh):
    assert mesh.shape["blk"] == ZS and mesh.shape["ulysses"] == XS * CORES
    tokens = P(("dp", "blk", "ulysses"), None)
    text = P(("dp", "ulysses"), None)
    return jax.shard_map(
        on_device,
        mesh=mesh,
        in_specs=(tokens, tokens, tokens, text, text, text, P("dp")),
        out_specs=(tokens, tokens),
        check_vma=False,
    )
```
